128 devices in a mesh: dp: 4 (over y), ctx: 32 (over x, z, core).
Axes of the slice: x: 4, y: 4, z: 4, core: 2. Of those that a mesh axis runs over, the one named last changes fastest.
Arguments:
- queries: bfloat16 [4, 6144, 8192], P('dp', 'ctx'), may hold values from -7 to 7
- keys: bfloat16 [4, 6144, 512], P('dp', 'ctx'), may hold values from -7 to 7
- values: bfloat16 [4, 6144, 512], P('dp', 'ctx'), may hold values from -6 to 6
- targets: bfloat16 [4, 6144, 8192], P('dp', 'ctx'), may hold values from -6 to 6
- segments: int32 [4, 6144], P('dp', 'ctx'), may hold values from 0 to 3, never falling along the last dimension, each value on 1 to 3072 neighbouring positions
- window: int32 [4], replicated, may hold values from 32 to 64, as said below
- query_feature_projection: bfloat16 [64, 128, 128], replicated, may hold values from -0.35 to 0.35
- key_map: bfloat16 [4, 128, 128], replicated, may hold values from -0.35 to 0.35
Outputs:
- grad_query_map: float32 [64, 128, 128], P('ctx')
- grad_key_map: float32 [4, 128, 128], replicated
The draws below stay inside these ranges and needn't reach their ends.
Inputs may be any that keep to these rules, and one draw needn't show every extreme that they name: `segments`: document numbers never fall along a sequence; each document has 1 to 3072 positions, and some document exactly 3072. Some head has a window of exactly 64.
All inputs are finite; a program needn't handle non-finite values.
Results may differ from the reference program's by a relative error of at most 0.0006.
Values may be sent and summed in bfloat16 or wider, within the bound.
No kernel may reach another device: no remote copies, remote signals or barrier semaphores. Data moves between devices by JAX's collectives and lax.ppermute only.
A program may use at most 192 MiB of HBM per device.

```python
import math
import jax
import jax.numpy as jnp
import numpy as np
from jax import lax

QUERY_HEADS = 64
KEY_VALUE_HEADS = 4
HEAD_SIZE = 128
FEATURE_COLUMNS = 128
WINDOW_LIMIT = 64
TOK_DEV = 192
SEQUENCE_BATCH = 4
SEQUENCE_LENGTH = 6144


def draw_queries(key, part):
    key = jax.random.fold_in(key, 3)
    tensor_dimensions = (SEQUENCE_BATCH, SEQUENCE_LENGTH, QUERY_HEADS, HEAD_SIZE)
    sampled_values = jnp.clip(jax.random.normal(key, tensor_dimensions, jnp.float32), -6.0, 6.0)
    return sampled_values.reshape(SEQUENCE_BATCH, SEQUENCE_LENGTH, QUERY_HEADS * HEAD_SIZE).astype(jnp.bfloat16)


def draw_keys(key, part):
    key = jax.random.fold_in(key, 5)
    tensor_dimensions = (SEQUENCE_BATCH, SEQUENCE_LENGTH, KEY_VALUE_HEADS, HEAD_SIZE)
    sampled_values = jnp.clip(jax.random.normal(key, tensor_dimensions, jnp.float32), -6.0, 6.0)
    return sampled_values.reshape(SEQUENCE_BATCH, SEQUENCE_LENGTH, KEY_VALUE_HEADS * HEAD_SIZE).astype(jnp.bfloat16)


def draw_query_feature_projection(key, part):
    key = jax.random.fold_in(key, 7)
    tensor_dimensions = (QUERY_HEADS, HEAD_SIZE, FEATURE_COLUMNS)
    sampled_values = jnp.clip(jax.random.normal(key, tensor_dimensions, jnp.float32) * HEAD_SIZE ** (-0.5), -0.35, 0.35)
    return sampled_values.astype(jnp.bfloat16)


def draw_key_map(key, part):
    key = jax.random.fold_in(key, 9)
    tensor_dimensions = (KEY_VALUE_HEADS, HEAD_SIZE, FEATURE_COLUMNS)
    sampled_values = jnp.clip(jax.random.normal(key, tensor_dimensions, jnp.float32) * HEAD_SIZE ** (-0.5), -0.35, 0.35)
    return sampled_values.astype(jnp.bfloat16)


def draw_window(key, part):
    key = jax.random.fold_in(key, 11)
    window_width_key, picked_random_key = jax.random.split(key)
    window_widths = jax.random.randint(window_width_key, (KEY_VALUE_HEADS,), WINDOW_LIMIT // 2, WINDOW_LIMIT + 1)
    picked_entries = jax.random.randint(picked_random_key, (), 0, KEY_VALUE_HEADS)
    return jnp.where(jnp.arange(KEY_VALUE_HEADS, dtype=jnp.int32) == picked_entries, WINDOW_LIMIT, window_widths).astype(jnp.int32)


def steps_of(stream_key, dims, shards, least, largest):
    level = 1.0
    for axis_at, parts in shards:
        steps = jax.random.uniform(jax.random.fold_in(jax.random.fold_in(stream_key, 6), axis_at), (parts,), jnp.float32, least / len(shards), largest / len(shards))
        level = level * jnp.repeat(jnp.exp(steps), dims[axis_at] // parts).reshape((-1,) + (1,) * (len(dims) - 1 - axis_at))
    return level


def split_up(amount, total, reach, slope):
    weights = [(1 << 20) // math.isqrt(grade ** slope) + 1 for grade in range(2, amount + 1)]
    rest, holding = total - reach - (amount - 1), [1] * (amount - 1)
    while rest > 0:
        candidates = [i for i in range(amount - 1) if holding[i] < reach]
        whole, remaining = sum([weights[i] for i in candidates]), rest
        for i in candidates:
            extra = min(reach - holding[i], max(1, remaining * weights[i] // whole), rest)
            holding[i] = holding[i] + extra
            rest = rest - extra
    return np.array([reach] + holding)


def uneven_parts(key, number_of, total, limit, slope):
    if number_of == 2:
        one = jax.random.randint(key, (), max(1, total - limit), min(limit, total - 1) + 1)
        return jnp.stack([one, total - one])
    tallies = jnp.asarray(split_up(number_of, total, limit, slope), jnp.int32)
    couples = (number_of - 1) // 2
    source_of, receiver = tallies[1:1 + 2 * couples:2], tallies[2:2 + 2 * couples:2]
    room = jnp.minimum(source_of - 1, limit - receiver)
    moved = jax.random.randint(jax.random.fold_in(key, 1), (couples,), 0, 1 << 20) % (room + 1)
    tallies = tallies.at[1:1 + 2 * couples:2].set(source_of - moved).at[2:2 + 2 * couples:2].set(receiver + moved)
    return tallies[jax.random.permutation(jax.random.fold_in(key, 2), number_of)]


def gaussian(rng, dims, scale, bound, pieces=(), held_as=jnp.bfloat16):
    result = jax.random.normal(rng, dims, jnp.float32) * scale
    if len(pieces) > 0:
        result = steps_of(rng, dims, pieces, -0.22, 0.18) * result
    return jnp.clip(result, min=-bound, max=bound).astype(held_as)


def setup_inputs(seed: int = 0) -> dict:
    seeds = jax.random.split(jax.random.key(seed), 9)
    return {
        "queries": draw_queries(jax.random.fold_in(seeds[8], 71), 0),
        "keys": draw_keys(jax.random.fold_in(seeds[8], 71), 0),
        "values": gaussian(seeds[2], (SEQUENCE_BATCH, SEQUENCE_LENGTH, KEY_VALUE_HEADS * HEAD_SIZE), 1.0, 6.0, ((0, 4), (1, 32))),
        "targets": gaussian(seeds[3], (SEQUENCE_BATCH, SEQUENCE_LENGTH, QUERY_HEADS * HEAD_SIZE), 1.0, 6.0, ((0, 4), (1, 32))),
        "segments": jax.vmap(lambda own: jnp.searchsorted(jnp.cumsum(uneven_parts(own, 4, SEQUENCE_LENGTH, SEQUENCE_LENGTH // 2, 0)), jnp.arange(SEQUENCE_LENGTH), side="right"))(jax.random.split(seeds[4], SEQUENCE_BATCH)).reshape((SEQUENCE_BATCH, SEQUENCE_LENGTH)).astype(jnp.int32),
        "window": draw_window(jax.random.fold_in(seeds[8], 71), 0),
        "query_feature_projection": draw_query_feature_projection(jax.random.fold_in(seeds[8], 71), 0),
        "key_map": draw_key_map(jax.random.fold_in(seeds[8], 71), 0),
    }


def feature_map(logits):
    return jnp.concatenate([jax.nn.softmax(logits, axis=-1), jax.nn.softmax(-logits, axis=-1)], axis=-1)

def sequence_loss(query_weight_matrix, key_weights, row_queries, row_keys, row_values, row_targets, segment_ids, window):
    query_group_size = QUERY_HEADS // KEY_VALUE_HEADS
    blocks = SEQUENCE_LENGTH // TOK_DEV
    near_rows = TOK_DEV + WINDOW_LIMIT
    highest = lax.Precision.HIGHEST
    head_queries = row_queries.astype(jnp.float32).reshape(SEQUENCE_LENGTH, KEY_VALUE_HEADS, query_group_size, HEAD_SIZE)
    head_targets = row_targets.astype(jnp.float32).reshape(SEQUENCE_LENGTH, KEY_VALUE_HEADS, query_group_size, HEAD_SIZE)
    head_keys = jnp.concatenate([jnp.zeros((WINDOW_LIMIT, KEY_VALUE_HEADS, HEAD_SIZE), jnp.float32), row_keys.astype(jnp.float32).reshape(SEQUENCE_LENGTH, KEY_VALUE_HEADS, HEAD_SIZE)], 0)
    head_values = jnp.concatenate([jnp.zeros((WINDOW_LIMIT, KEY_VALUE_HEADS, HEAD_SIZE), jnp.float32), row_values.astype(jnp.float32).reshape(SEQUENCE_LENGTH, KEY_VALUE_HEADS, HEAD_SIZE)], 0)
    padded_segments = jnp.concatenate([jnp.full((WINDOW_LIMIT,), -1, jnp.int32), segment_ids.astype(jnp.int32)], 0)
    key_logits = jnp.einsum('ngd,gdf->gnf', head_keys, key_weights, precision=highest)
    key_features = feature_map(key_logits)

    def block_loss(state_carry, block_index):
        prefix_state, prefix_norm = state_carry
        offset = (block_index * TOK_DEV).astype(jnp.int32)
        query_block = lax.dynamic_slice_in_dim(head_queries, offset, TOK_DEV, 0)
        target_block = lax.dynamic_slice_in_dim(head_targets, offset, TOK_DEV, 0)
        near_keys = lax.dynamic_slice_in_dim(head_keys, offset, near_rows, 0)
        near_values = lax.dynamic_slice_in_dim(head_values, offset, near_rows, 0)
        near_features = lax.dynamic_slice_in_dim(key_features, offset, near_rows, 1)
        near_segments = lax.dynamic_slice_in_dim(padded_segments, offset, near_rows, 0)
        block_segments = near_segments[WINDOW_LIMIT:]
        positions = offset + jnp.arange(TOK_DEV, dtype=jnp.int32)
        near_positions = offset - WINDOW_LIMIT + jnp.arange(near_rows, dtype=jnp.int32)
        query_logits = jnp.einsum('ighd,ghdf->ighf', query_block, query_weight_matrix, precision=highest)
        query_features = feature_map(query_logits)
        scores = jnp.einsum('ighd,jgd->ighj', query_block, near_keys, precision=highest) * HEAD_SIZE ** (-0.5)
        same_doc = block_segments[:, None] == near_segments[None, :]
        distance = positions[:, None] - near_positions[None, :]
        window_reach = window.astype(jnp.int32)[None, :, None]
        in_window = same_doc[:, None, :] & (distance[:, None, :] >= 0) & (distance[:, None, :] < window_reach)
        own_far = same_doc[:, None, :] & (near_positions >= offset)[None, None, :] & (distance[:, None, :] >= window_reach)
        rim_near = same_doc[:, None, :] & (near_positions < offset)[None, None, :] & (distance[:, None, :] < window_reach)
        signed_mask = own_far.astype(jnp.float32) - rim_near.astype(jnp.float32)
        window_mask = in_window[:, :, None, :]
        window_max = lax.optimization_barrier(jnp.max(jnp.where(window_mask, scores, -jnp.inf), axis=-1, keepdims=True))
        window_weights = jnp.where(window_mask, jnp.exp(jnp.where(window_mask, scores - window_max, 0.0)), 0.0)
        linear_weights = jnp.einsum('ighf,gjf->ighj', query_features, near_features, precision=highest) * signed_mask[:, :, None, :]
        prev_last = near_segments[WINDOW_LIMIT - 1]
        carried = (block_segments == prev_last).astype(jnp.float32)[:, None, None]
        all_weights = window_weights + linear_weights
        numerator = jnp.einsum('ighj,jgd->ighd', all_weights, near_values, precision=highest)
        numerator = numerator + carried[..., None] * jnp.einsum('ighf,gfd->ighd', query_features, prefix_state, precision=highest)
        denominator = lax.optimization_barrier(jnp.sum(all_weights, axis=-1)) + carried * jnp.einsum('ighf,gf->igh', query_features, prefix_norm, precision=highest)
        outputs = numerator / denominator[..., None]
        block_value = 0.5 * jnp.sum((outputs - target_block) ** 2)
        seg_last = block_segments[TOK_DEV - 1]
        keep_factor = (prev_last == seg_last).astype(jnp.float32)
        tail_mask = (block_segments == seg_last).astype(jnp.float32)
        own_features = near_features[:, WINDOW_LIMIT:] * tail_mask[None, :, None]
        own_values = near_values[WINDOW_LIMIT:]
        new_state = keep_factor * prefix_state + jnp.einsum('gjf,jgd->gfd', own_features, own_values, precision=highest)
        new_norm = keep_factor * prefix_norm + lax.optimization_barrier(jnp.sum(own_features, axis=1))
        return ((new_state, new_norm), block_value)
    starting_value = (jnp.zeros((KEY_VALUE_HEADS, 2 * FEATURE_COLUMNS, HEAD_SIZE), jnp.float32), jnp.zeros((KEY_VALUE_HEADS, 2 * FEATURE_COLUMNS), jnp.float32))
    final_state, losses = lax.scan(jax.checkpoint(block_loss), starting_value, jnp.arange(blocks, dtype=jnp.int32))
    return jnp.sum(losses)

def reference(queries, keys, values, targets, segments, window, query_feature_projection, key_map):
    query_weight_matrix = query_feature_projection.astype(jnp.float32).reshape(KEY_VALUE_HEADS, QUERY_HEADS // KEY_VALUE_HEADS, HEAD_SIZE, FEATURE_COLUMNS)
    key_weights = key_map.astype(jnp.float32)
    gradient_fn = jax.grad(sequence_loss, argnums=(0, 1))
    combined_query = jnp.zeros((KEY_VALUE_HEADS, QUERY_HEADS // KEY_VALUE_HEADS, HEAD_SIZE, FEATURE_COLUMNS), jnp.float32)
    combined_key = jnp.zeros((KEY_VALUE_HEADS, HEAD_SIZE, FEATURE_COLUMNS), jnp.float32)
    for sequence in range(SEQUENCE_BATCH):
        query_part, key_part = gradient_fn(query_weight_matrix, key_weights, queries[sequence], keys[sequence], values[sequence], targets[sequence], segments[sequence], window)
        combined_query = combined_query + query_part
        combined_key = combined_key + key_part
    return (combined_query.reshape(QUERY_HEADS, HEAD_SIZE, FEATURE_COLUMNS), combined_key)
```

```python
import functools
import jax
import jax.numpy as jnp
from jax import lax
from jax.experimental import pallas as pl
from jax.experimental.pallas import tpu as pltpu
from jax.sharding import PartitionSpec as P

CHUNK = 64
QUAD = 4
LANES = QUAD * CHUNK
NEAR = 2 * CHUNK
MASKED = -1e30
F32 = jnp.float32
BF16 = jnp.bfloat16
VMEM_LIMIT = 60 * 1024 * 1024


def halves(x):
    high = x.astype(BF16)
    return high, (x - high.astype(F32)).astype(BF16)


def mm(a, b):
    return jnp.dot(a, b, preferred_element_type=F32)


def mm_nt(a, b):
    return lax.dot_general(a, b, (((1,), (1,)), ((), ())), preferred_element_type=F32)


def softmaxes(logits, axis):
    upper = jnp.exp(logits - jnp.max(logits, axis=axis, keepdims=True))
    lower = jnp.exp(jnp.min(logits, axis=axis, keepdims=True) - logits)
    return (
        upper * (1.0 / jnp.sum(upper, axis=axis, keepdims=True)),
        lower * (1.0 / jnp.sum(lower, axis=axis, keepdims=True)),
    )


def softmax_grads(upper, lower, grad_upper, grad_lower, axis):
    return upper * (
        grad_upper - jnp.sum(upper * grad_upper, axis=axis, keepdims=True)
    ) - lower * (grad_lower - jnp.sum(lower * grad_lower, axis=axis, keepdims=True))


def keep(seg_ref, chunk):
    same = seg_ref[CHUNK * (chunk + 1) - 1] == seg_ref[CHUNK * (chunk + 2) - 1]
    return jnp.where(same, 1.0, 0.0).astype(F32)


def side(first, count, piece):
    return piece[:, first : first + count].reshape(-1, piece.shape[2])


def block_kernel(
    chunks, seg_ref, key_ref, value_ref, map_ref, seg_row_ref, state_ref, piece_ref
):
    upper, lower = softmaxes(mm(key_ref[...], map_ref[0]), 1)
    high, low = halves(jnp.concatenate([upper, lower], 1))
    values = value_ref[...].astype(F32)
    total = None
    for c in range(chunks):
        own = slice(CHUNK * c, CHUNK * (c + 1))
        tail = seg_row_ref[c, :, :CHUNK] == seg_ref[CHUNK * (c + 1) - 1]
        turned = jnp.concatenate([values[own].T, jnp.ones((16, CHUNK), F32)], 0)
        turned = jnp.where(tail, turned, 0.0).astype(BF16)
        state = mm(
            jnp.concatenate([turned, turned], 1), jnp.concatenate([high[own], low[own]], 0)
        )[: state_ref.shape[2]]
        state_ref[0, c] = state
        total = state if c == 0 else state + keep(seg_ref, c - 1) * total
    cut_up(total, seg_ref, piece_ref)


def key_kernel(
    chunks, window_ref, key_ref, value_ref, map_ref, seg_col_ref, seg_row_ref,
    feat_high_ref, feat_low_ref, feat_t_ref, value_t_ref, value_pair_ref, bias_ref, sign_ref,
):
    reach = window_ref[pl.program_id(0)]
    upper, lower = softmaxes(mm(key_ref[...], map_ref[0]), 1)
    features = jnp.concatenate([upper, lower], 1)
    high, low = halves(features)
    feat_high_ref[0] = high
    feat_low_ref[0] = low
    values = value_ref[...]
    value_pair_ref[0] = jnp.concatenate([values, values], 1)
    wide_values = values.astype(F32)
    for c in range(chunks):
        rows = slice(CHUNK * c, CHUNK * c + NEAR)
        turned_high, turned_low = halves(features[rows].T)
        feat_t_ref[0, c] = jnp.concatenate([turned_high, turned_low], 1)
        value_t = wide_values[rows].T.astype(BF16)
        value_t_ref[0, c] = jnp.concatenate([value_t, value_t], 1)
        near_row = lax.broadcasted_iota(jnp.int32, (NEAR, LANES), 0)
        token = lax.broadcasted_iota(jnp.int32, (NEAR, LANES), 1) % CHUNK
        distance = CHUNK + token - near_row
        same_doc = seg_col_ref[rows] == seg_row_ref[c]
        inside = distance < reach
        in_window = same_doc & (distance >= 0) & inside
        bias_ref[0, c] = jnp.where(in_window, 0.0, MASKED).astype(F32)
        far = same_doc & (near_row >= CHUNK) & (distance >= reach)
        rim = same_doc & (near_row < CHUNK) & inside
        sign_ref[0, c] = jnp.where(far, 1.0, jnp.where(rim, -1.0, 0.0)).astype(F32)


def cut_up(total, seg_ref, piece_ref):
    share = piece_ref.shape[1] - 8
    width = total.shape[1]
    end = seg_ref[seg_ref.shape[0] - 1].astype(F32)
    extra = jnp.where(
        lax.broadcasted_iota(jnp.int32, (8, width), 0) == 0, total[128:136], end
    )
    for i in range(piece_ref.shape[0]):
        piece_ref[i, :share] = total[share * i : share * (i + 1)]
        piece_ref[i, share:] = extra


def whole_state(piece):
    share = piece.shape[1] - 8
    state = side(0, share, piece)
    norm = jnp.broadcast_to(piece[0, share : share + 1], (8, piece.shape[2]))
    return jnp.concatenate([state, norm], 0)


def scan_kernel(count, backward, piece_ref, out_ref):
    mark = piece_ref.shape[1] - 7
    total = jnp.zeros(piece_ref.shape[1:], F32)
    for position in range(count - 1, -1, -1) if backward else range(count):
        out_ref[position] = total
        piece = piece_ref[position]
        former = piece_ref[max(position - 1, 0), mark : mark + 1]
        total = piece + jnp.where(piece[mark : mark + 1] == former, total, 0.0)


def place_diagonal(blocks, diag_ref):
    for i, block in enumerate(blocks):
        diag_ref[i * CHUNK : (i + 1) * CHUNK, i * 128 : (i + 1) * 128] = block


def local_kernel(
    chunks, q0_ref, q1_ref, q2_ref, q3_ref, m0_ref, m1_ref, m2_ref, m3_ref, key_ref, high_ref,
    low_ref, value_t_ref, bias_ref, sign_ref, *refs,
):
    numer_ref, denom_ref, qf_high_ref, qf_low_ref, diag_ref = refs[-5:]

    @pl.when(pl.program_id(0) + pl.program_id(1) == 0)
    def _():
        diag_ref[...] = jnp.zeros_like(diag_ref)

    q_refs = (q0_ref, q1_ref, q2_ref, q3_ref)
    maps = jnp.concatenate([ref[0] for ref in (m0_ref, m1_ref, m2_ref, m3_ref)], 0)
    maps = maps.astype(F32).T.astype(BF16)
    every = range(chunks)
    near = [slice(CHUNK * c, CHUNK * c + NEAR) for c in every]
    blocks = [[ref[CHUNK * c : CHUNK * (c + 1)] for ref in q_refs] for c in every]
    for c in every:
        place_diagonal(blocks[c], diag_ref.at[c])
    logits = [mm_nt(maps, diag_ref[c]) for c in every]
    scores = [mm_nt(key_ref[near[c]], jnp.concatenate(blocks[c], 0)) for c in every]
    for c in every:
        upper, lower = softmaxes(logits[c], 0)
        high, low = halves(jnp.concatenate([upper, lower], 0))
        qf_high_ref[0, c] = high
        qf_low_ref[0, c] = low
        score = scores[c] * 128 ** (-0.5) + bias_ref[0, c]
        weights = jnp.exp(score - jnp.max(score, axis=0, keepdims=True))
        key_high = high_ref[0, near[c]]
        both = mm(jnp.concatenate([key_high, low_ref[0, near[c]]], 0), high)
        linear = both[:NEAR] + both[NEAR:] + mm(key_high, low)
        weights = weights + linear * sign_ref[0, c]
        denom_ref[0, c] = jnp.sum(weights, axis=0, keepdims=True)
        numer_ref[0, c] = mm(value_t_ref[0, c], jnp.concatenate(halves(weights), 0))


def enter_states(chunks, seg_ref, first_ref, state_ref, feat_t_ref, rows_ref, columns_ref, norm_ref):
    state = whole_state(first_ref)
    for c in range(chunks):
        if c > 0:
            state = state_ref[0, c - 1] + keep(seg_ref, c - 1) * state
        high, low = halves(jnp.concatenate([state, state[128:]], 0))
        rows_ref[c] = jnp.concatenate([high, low], 0)
        turned_high, turned_low = halves(state[:128].T)
        feat_high, feat_low = feat_t_ref[0, c, :, :NEAR], feat_t_ref[0, c, :, NEAR:]
        columns_ref[0, c] = jnp.concatenate(
            [feat_high, feat_high, turned_high, turned_high, feat_low, turned_low], 1
        )
        norm_ref[0, c] = jnp.broadcast_to(state[128:129], (128, state.shape[1])).T


def output_kernel(
    chunks, seg_ref, t0_ref, t1_ref, t2_ref, t3_ref, numer_ref, denom_ref, qf_high_ref, qf_low_ref,
    first_ref, state_ref, feat_t_ref, value_pair_ref, sign_ref, seg_row_ref, right_ref,
    grad_denom_ref, key_grad_ref, state_grad_ref, piece_ref, columns_ref, norm_ref, rows_ref,
):
    begins = pl.program_id(1) + pl.program_id(2) == 0
    ends = (pl.program_id(1) == 1) & (pl.program_id(2) == pl.num_programs(2) - 1)

    @pl.when(begins)
    def _():
        enter_states(
            chunks, seg_ref, first_ref, state_ref, feat_t_ref, rows_ref, columns_ref, norm_ref
        )

    t_refs = (t0_ref, t1_ref, t2_ref, t3_ref)
    padded = rows_ref.shape[1] // 2
    results = []
    for c in range(chunks):
        carried = jnp.where(seg_row_ref[c] == seg_ref[c * CHUNK + CHUNK - 1], 1.0, 0.0).astype(F32)
        high, low = qf_high_ref[0, c], qf_low_ref[0, c]
        both = mm(rows_ref[c], high)
        carry = both[:padded] + both[padded:] + mm(rows_ref[c, :padded], low)
        carry = carry * carried
        inverse = 1.0 / (denom_ref[0, c] + carry[128:129])
        outputs = (numer_ref[0, c] + carry[:128]) * inverse
        targets = jnp.concatenate([ref[CHUNK * c : CHUNK * (c + 1)] for ref in t_refs], 0)
        residual = outputs - targets.astype(F32).T
        grad = residual * inverse
        grad_denom = -jnp.sum(residual * outputs, axis=0, keepdims=True) * inverse
        grad_denom_ref[0, c] = grad_denom * carried
        grad_high, grad_low = halves(grad)
        near = slice(CHUNK * c, CHUNK * c + NEAR)
        linear = mm(value_pair_ref[0, near], jnp.concatenate([grad_high, grad_low], 0))
        linear_high, linear_low = halves((linear + grad_denom) * sign_ref[0, c])
        mask = carried.astype(BF16)
        grad_high, grad_low = grad_high * mask, grad_low * mask
        right_ref[0, c] = jnp.concatenate([linear_high, linear_low, grad_high, grad_low], 0)
        denom_high, denom_low = halves(jnp.broadcast_to(grad_denom * carried, (16, LANES)))
        left_high = jnp.concatenate([linear_high, grad_high, denom_high], 0)
        left_low = jnp.concatenate([linear_low, grad_low, denom_low], 0)
        both = mm_nt(jnp.concatenate([left_high, left_low], 0), high)
        rows = left_high.shape[0]
        results.append(both[:rows] + both[rows:] + mm_nt(left_high, low))

    @pl.when(begins)
    def _():
        for c in range(chunks):
            key_grad_ref[0, c] = results[c][:NEAR]
            state_grad_ref[0, c] = results[c][NEAR : NEAR + 136]

    @pl.when(jnp.logical_not(begins))
    def _():
        for c in range(chunks):
            key_grad_ref[0, c] += results[c][:NEAR]
            state_grad_ref[0, c] += results[c][NEAR : NEAR + 136]

    @pl.when(ends)
    def _():
        total = state_grad_ref[0, chunks - 1]
        for c in range(chunks - 2, -1, -1):
            total = state_grad_ref[0, c] + keep(seg_ref, c) * total
        cut_up(total, seg_ref, piece_ref)


def query_kernel(
    chunks, core_ref, q0_ref, q1_ref, q2_ref, q3_ref, right_ref, grad_denom_ref, qf_high_ref,
    qf_low_ref, columns_ref, norm_ref, mine_ref, theirs_ref, diag_ref,
):
    @pl.when(pl.program_id(0) + pl.program_id(1) == 0)
    def _():
        diag_ref[...] = jnp.zeros_like(diag_ref)

    q_refs = (q0_ref, q1_ref, q2_ref, q3_ref)
    for c in range(chunks):
        place_diagonal([ref[CHUNK * c : CHUNK * (c + 1)] for ref in q_refs], diag_ref.at[c])
    total = None
    for c in range(chunks):
        stack = right_ref[0, c]
        right = jnp.concatenate([stack, stack[:NEAR], stack[2 * NEAR : 2 * NEAR + 128]], 0)
        norm = jnp.concatenate([norm_ref[0, c]] * (LANES // 128), 1)
        feature_grad = mm(columns_ref[0, c], right) + norm * grad_denom_ref[0, c]
        high, low = qf_high_ref[0, c], qf_low_ref[0, c]
        upper = high[:128].astype(F32) + low[:128].astype(F32)
        lower = high[128:].astype(F32) + low[128:].astype(F32)
        logit_grad = softmax_grads(upper, lower, feature_grad[:128], feature_grad[128:], 0)
        both = mm(jnp.concatenate(halves(logit_grad), 0), diag_ref[c])
        query_grad = both[:128] + both[128:]
        total = query_grad if total is None else total + query_grad

    share = mine_ref.shape[2]
    for core, own in enumerate(((mine_ref, theirs_ref), (theirs_ref, mine_ref))):

        @pl.when(core_ref[0] == core)
        def _(own=own):
            for k in range(mine_ref.shape[0]):
                for i in range(QUAD):
                    own[i % 2][k, i // 2] = total[
                        share * k : share * (k + 1), i * 128 : (i + 1) * 128
                    ]


def tail_kernel(
    chunks, seg_ref, key_ref, value_ref, map_ref, seg_col_ref, later_ref, state_grad_ref,
    key_grad_ref, out_ref,
):
    logits = mm(key_ref[...], map_ref[0])
    upper, lower = softmaxes(logits, 1)
    values = value_ref[...]
    pieces = [key_grad_ref[0, 0, :CHUNK]]
    leaving = whole_state(later_ref)
    states = []
    for c in range(chunks - 1, -1, -1):
        states.append(leaving)
        leaving = state_grad_ref[0, c] + keep(seg_ref, c) * leaving
    states = states[::-1]
    for c in range(chunks):
        own = slice(CHUNK * (c + 1), CHUNK * (c + 2))
        grads = key_grad_ref[0, c, CHUNK:]
        if c + 1 < chunks:
            grads = grads + key_grad_ref[0, c + 1, :CHUNK]
        tail = jnp.where(seg_col_ref[own] == seg_ref[CHUNK * (c + 2) - 1], 1.0, 0.0).astype(F32)
        entry_high, entry_low = halves(states[c][:128])
        through = mm(
            jnp.concatenate([values[own], values[own]], 1),
            jnp.concatenate([entry_high, entry_low], 0),
        )
        pieces.append(grads + tail * (through + states[c][128:129]))
    grads = jnp.concatenate(pieces, 0)
    logit_grad = softmax_grads(upper, lower, grads[:, :128], grads[:, 128:], 1)
    turned = key_ref[...].astype(F32).T.astype(BF16)
    out_ref[0] = mm(
        jnp.concatenate([turned, turned], 1), jnp.concatenate(halves(logit_grad), 0)
    )


def call(
    kernel, name, microseconds, grid, in_specs, out_specs, out_shape, args, scalars=0, scratch=(),
    aliases=None,
):
    return pl.pallas_call(
        kernel,
        grid_spec=pltpu.PrefetchScalarGridSpec(
            num_scalar_prefetch=scalars,
            grid=grid,
            in_specs=in_specs,
            out_specs=out_specs,
            scratch_shapes=scratch,
        ),
        out_shape=out_shape,
        compiler_params=pltpu.CompilerParams(vmem_limit_bytes=VMEM_LIMIT),
        cost_estimate=pl.CostEstimate(
            flops=int(microseconds * 1e9), bytes_accessed=int(microseconds * 3e6), transcendentals=0
        ),
        input_output_aliases=aliases or {},
        name=name,
    )(*args)


def exchange(pieces, axis):
    return lax.all_to_all(pieces, axis, 0, 0, tiled=True)


def on_device(queries, keys, values, targets, segments, window, query_feature_projection, key_map):
    head_count, head_dim, map_width = query_feature_projection.shape
    groups = key_map.shape[0]
    tok_rows = queries.shape[1]
    near_rows = tok_rows + CHUNK
    chunks = tok_rows // CHUNK
    features = 2 * map_width
    quads = head_count // groups // QUAD // 2
    ctx, dp = lax.axis_size("ctx"), lax.axis_size("dp")
    me = lax.axis_index("ctx")
    state_rows = head_dim + 8
    sds = jax.ShapeDtypeStruct

    seg_row = segments[0]
    seg_rows = jnp.tile(seg_row.reshape(chunks, 1, CHUNK), (1, 1, QUAD))
    query_rows, target_rows = queries[0], targets[0]
    group_spec = lambda *shape: pl.BlockSpec((1,) + shape, lambda g, *_: (g,) + (0,) * len(shape))
    whole = lambda shape: pl.BlockSpec(shape, lambda *_: (0,) * len(shape))
    column = lambda rows: pl.BlockSpec((rows, head_dim), lambda g, *_: (0, g))
    per_group = ctx // groups
    piece_shape = (ctx, head_dim // per_group + 8, features)
    piece_spec = pl.BlockSpec((per_group,) + piece_shape[1:], lambda g, *_: (g, 0, 0))

    chunk_state, block_pieces = call(
        functools.partial(block_kernel, chunks), "block", 4, (groups,),
        [
            column(tok_rows), column(tok_rows), group_spec(head_dim, map_width),
            whole((chunks, 1, LANES)),
        ],
        [group_spec(chunks, state_rows, features), piece_spec],
        [sds((groups, chunks, state_rows, features), F32), sds(piece_shape, F32)],
        (seg_row, keys[0], values[0], key_map, seg_rows),
        scalars=1,
    )

    def across(pieces, backward, beside=lambda: ()):
        received, aside = exchange(pieces, "ctx"), beside()
        received, aside = lax.optimization_barrier((received, aside))
        summed = call(
            functools.partial(scan_kernel, ctx, backward), "scan", 2, (1,), [whole(piece_shape)],
            whole(piece_shape), sds(piece_shape, F32), (received,),
        )
        return exchange(summed, "ctx"), aside

    rim = jnp.concatenate([keys[0, -CHUNK:], values[0, -CHUNK:]], 1)
    rim_seg = jnp.broadcast_to(seg_row[-CHUNK:].astype(BF16)[:, None], (CHUNK, 128))
    rim = lax.ppermute(
        jnp.concatenate([rim, rim_seg], 1), "ctx", [(i, i + 1) for i in range(ctx - 1)]
    )
    width = keys.shape[2]
    near_keys = jnp.concatenate([rim[:, :width], keys[0]], 0)
    near_values = jnp.concatenate([rim[:, width : 2 * width], values[0]], 0)
    rim_segments = jnp.where(me > 0, rim[:, 2 * width].astype(jnp.int32), -1)
    near_segments = jnp.concatenate([rim_segments, seg_row], 0)
    seg_col = near_segments[:, None]
    feat_high, feat_low, feat_t, value_t, value_pair, bias, sign = call(
        functools.partial(key_kernel, chunks), "keys", 5, (groups,),
        [
            column(near_rows), column(near_rows), group_spec(head_dim, map_width),
            whole((near_rows, 1)), whole((chunks, 1, LANES)),
        ],
        [
            group_spec(near_rows, features), group_spec(near_rows, features),
            group_spec(chunks, features, 2 * NEAR), group_spec(chunks, head_dim, 2 * NEAR),
            group_spec(near_rows, 2 * head_dim), group_spec(chunks, NEAR, LANES),
            group_spec(chunks, NEAR, LANES),
        ],
        [
            sds((groups, near_rows, features), BF16), sds((groups, near_rows, features), BF16),
            sds((groups, chunks, features, 2 * NEAR), BF16),
            sds((groups, chunks, head_dim, 2 * NEAR), BF16),
            sds((groups, near_rows, 2 * head_dim), BF16),
            sds((groups, chunks, NEAR, LANES), F32), sds((groups, chunks, NEAR, LANES), F32),
        ],
        (window, near_keys, near_values, key_map, seg_col, seg_rows),
        scalars=1,
    )

    half_steps = groups * quads
    steps = 2 * half_steps
    grid = (groups, quads)
    spot = lambda g, q: g * quads + q

    def step_spec(half, *shape):
        return pl.BlockSpec(
            (1,) + shape, lambda g, q, *_: (half * half_steps + spot(g, q),) + (0,) * len(shape)
        )

    def head_specs(half):
        return [
            pl.BlockSpec(
                (tok_rows, head_dim), lambda g, q, *_, i=i: (0, (spot(g, q) * QUAD + i) * 2 + half)
            )
            for i in range(QUAD)
        ]

    def local(half, so_far):
        map_specs = [
            pl.BlockSpec(
                (1, head_dim, map_width),
                lambda g, q, *_, i=i: ((spot(g, q) * QUAD + i) * 2 + half, 0, 0),
            )
            for i in range(QUAD)
        ]
        step = functools.partial(step_spec, half)
        return call(
            functools.partial(local_kernel, chunks), "local", 15, grid,
            head_specs(half) + map_specs
            + [
                column(near_rows), group_spec(near_rows, features),
                group_spec(near_rows, features), group_spec(chunks, head_dim, 2 * NEAR),
                group_spec(chunks, NEAR, LANES), group_spec(chunks, NEAR, LANES),
            ]
            + [pl.BlockSpec(memory_space=pl.ANY)] * len(so_far),
            [
                step(chunks, head_dim, LANES), step(chunks, 1, LANES),
                step(chunks, features, LANES), step(chunks, features, LANES),
            ],
            [
                sds((steps, chunks, head_dim, LANES), F32), sds((steps, chunks, 1, LANES), F32),
                sds((steps, chunks, features, LANES), BF16),
                sds((steps, chunks, features, LANES), BF16),
            ],
            (
                *([query_rows] * QUAD), *([query_feature_projection] * QUAD), near_keys, feat_high,
                feat_low, value_t, bias, sign, *so_far,
            ),
            scratch=[pltpu.VMEM((chunks, LANES, QUAD * head_dim), BF16)],
            aliases={14 + i: i for i in range(len(so_far))},
        )

    entering, forward = across(block_pieces, False, lambda: local(0, ()))
    entering, forward = lax.optimization_barrier((entering, local(1, forward)))

    every_step = lambda *shape: pl.BlockSpec(
        (1,) + shape, lambda g, h, q, *_: (h * half_steps + spot(g, q),) + (0,) * len(shape)
    )
    right, grad_denom, key_grad, state_grad, grad_pieces, columns, norms = call(
        functools.partial(output_kernel, chunks), "outputs", 45, (groups, 2, quads),
        [
            pl.BlockSpec(
                (tok_rows, head_dim),
                lambda g, h, q, *_, i=i: (0, (spot(g, q) * QUAD + i) * 2 + h),
            )
            for i in range(QUAD)
        ]
        + [
            every_step(chunks, head_dim, LANES), every_step(chunks, 1, LANES),
            every_step(chunks, features, LANES), every_step(chunks, features, LANES),
            piece_spec, group_spec(chunks, state_rows, features),
            group_spec(chunks, features, 2 * NEAR), group_spec(near_rows, 2 * head_dim),
            group_spec(chunks, NEAR, LANES), whole((chunks, 1, LANES)),
        ],
        [
            every_step(chunks, 4 * NEAR, LANES), every_step(chunks, 1, LANES),
            group_spec(chunks, NEAR, features), group_spec(chunks, state_rows, features),
            piece_spec, group_spec(chunks, features, 6 * 128), group_spec(chunks, features, 128),
        ],
        [
            sds((steps, chunks, 4 * NEAR, LANES), BF16), sds((steps, chunks, 1, LANES), F32),
            sds((groups, chunks, NEAR, features), F32),
            sds((groups, chunks, state_rows, features), F32), sds(piece_shape, F32),
            sds((groups, chunks, features, 6 * 128), BF16),
            sds((groups, chunks, features, 128), F32),
        ],
        (
            near_segments, *([target_rows] * QUAD), *forward, entering, chunk_state, feat_t,
            value_pair, sign, seg_rows,
        ),
        scalars=1,
        scratch=[pltpu.VMEM((chunks, 2 * (state_rows + 8), features), BF16)],
    )

    core = lax.rem(me, 2)
    partner = [(i, i ^ 1) for i in range(ctx)]

    def query(half):
        share = map_width // dp
        step = functools.partial(step_spec, half)
        shape = (dp, head_count // 4, share, head_dim)
        part = pl.BlockSpec((dp, QUAD // 2, share, head_dim), lambda g, q, *_: (0, spot(g, q), 0, 0))
        mine, theirs = call(
            functools.partial(query_kernel, chunks), "queries", 15, grid,
            head_specs(half)
            + [
                step(chunks, 4 * NEAR, LANES), step(chunks, 1, LANES),
                step(chunks, features, LANES), step(chunks, features, LANES),
                group_spec(chunks, features, 6 * 128), group_spec(chunks, features, 128),
            ],
            [part, part], [sds(shape, F32), sds(shape, F32)],
            (core[None], *([query_rows] * QUAD), right, grad_denom, *forward[2:], columns, norms),
            scalars=1,
            scratch=[pltpu.VMEM((chunks, LANES, QUAD * head_dim), BF16)],
        )
        return (mine + lax.ppermute(theirs, "ctx", partner)).reshape(-1, share, head_dim)

    later, first = across(grad_pieces, True, lambda: query(0))
    later, second = lax.optimization_barrier((later, query(1)))

    key_grad = call(
        functools.partial(tail_kernel, chunks), "tail", 5, (groups,),
        [
            column(near_rows), column(near_rows), group_spec(head_dim, map_width),
            whole((near_rows, 1)), piece_spec, group_spec(chunks, state_rows, features),
            group_spec(chunks, NEAR, features),
        ],
        group_spec(head_dim, map_width), sds((groups, head_dim, map_width), F32),
        (
            near_segments, near_keys, near_values, key_map, seg_col, later, state_grad, key_grad,
        ),
        scalars=1,
    )

    everyone = ("dp", "ctx")
    devices = dp * ctx
    same_core = [[i for i in range(devices) if i % 2 == k] for k in range(2)]

    def summed(pieces):
        received = lax.all_to_all(
            pieces, everyone, 0, 0, tiled=True, axis_index_groups=same_core
        )
        return jnp.sum(received, axis=0)

    first = summed(first)
    key_halves = key_grad.reshape(2, -1, map_width)
    key_mine = lax.dynamic_index_in_dim(key_halves, core, 0, False)
    key_theirs = lax.dynamic_index_in_dim(key_halves, 1 - core, 0, False)
    key_mine = key_mine + lax.ppermute(key_theirs, "ctx", partner)
    rows = second.shape[1]
    second = summed(
        jnp.concatenate([second, key_mine.reshape(devices // 2, -1, map_width)], 1)
    )
    key_share = second[rows:]
    full_key = exchange(jnp.broadcast_to(key_share, (devices,) + key_share.shape), everyone)
    full_key = full_key.reshape(devices // 2, 2, -1, map_width).transpose(1, 0, 2, 3)
    full_key = full_key.reshape(groups, head_dim, map_width)
    own = jnp.stack([first, second[:rows]], 0)
    full_query = lax.all_gather(own, "dp", axis=1, tiled=True)
    return (full_query.transpose(0, 2, 1), full_key)


def solution(mesh):
    return jax.shard_map(
        on_device,
        mesh=mesh,
        in_specs=(
            P("dp", "ctx", None),
            P("dp", "ctx", None),
            P("dp", "ctx", None),
            P("dp", "ctx", None),
            P("dp", "ctx"),
            P(),
            P(),
            P(),
        ),
        out_specs=(P("ctx", None, None), P()),
        check_vma=False,
    )
```

```python
import functools
import jax
import jax.numpy as jnp
from jax import lax
from jax.experimental import pallas as pl
from jax.experimental.pallas import tpu as pltpu
from jax.sharding import PartitionSpec as P

CHUNK = 64
QUAD = 4
LANES = QUAD * CHUNK
NEAR = 2 * CHUNK
MASKED = -1e30
OWN_FAR, OWN_NEAR, RIM_NEAR = 1.0, 2.0, 3.0
F32 = jnp.float32
BF16 = jnp.bfloat16
RING = 4
VMEM_LIMIT = 60 * 1024 * 1024


def halves(x):
    high = x.astype(BF16)
    return high, (x - high.astype(F32)).astype(BF16)


def mm(a, b):
    return jnp.dot(a, b, preferred_element_type=F32)


def mm_nt(a, b):
    return lax.dot_general(a, b, (((1,), (1,)), ((), ())), preferred_element_type=F32)


def softmaxes(logits, axis):
    upper = jnp.exp(logits - jnp.max(logits, axis=axis, keepdims=True))
    lower = jnp.exp(jnp.min(logits, axis=axis, keepdims=True) - logits)
    return (
        upper * (1.0 / jnp.sum(upper, axis=axis, keepdims=True)),
        lower * (1.0 / jnp.sum(lower, axis=axis, keepdims=True)),
    )


def softmax_grads(upper, lower, grad_upper, grad_lower, axis):
    return upper * (
        grad_upper - jnp.sum(upper * grad_upper, axis=axis, keepdims=True)
    ) - lower * (grad_lower - jnp.sum(lower * grad_lower, axis=axis, keepdims=True))


def keep(seg_ref, chunk):
    same = seg_ref[CHUNK * (chunk + 1) - 1] == seg_ref[CHUNK * (chunk + 2) - 1]
    return jnp.where(same, 1.0, 0.0).astype(F32)


def side(first, count, piece):
    return piece[:, first : first + count].reshape(-1, piece.shape[2])


def block_kernel(
    chunks, seg_ref, key_ref, value_ref, map_ref, seg_row_ref, state_ref, piece_ref
):
    upper, lower = softmaxes(mm(key_ref[...], map_ref[0]), 1)
    high, low = halves(jnp.concatenate([upper, lower], 1))
    values = value_ref[...].astype(F32)
    total = None
    for c in range(chunks):
        own = slice(CHUNK * c, CHUNK * (c + 1))
        tail = seg_row_ref[c, :, :CHUNK] == seg_ref[CHUNK * (c + 1) - 1]
        turned = jnp.concatenate([values[own].T, jnp.ones((16, CHUNK), F32)], 0)
        turned = jnp.where(tail, turned, 0.0).astype(BF16)
        state = mm(
            jnp.concatenate([turned, turned], 1), jnp.concatenate([high[own], low[own]], 0)
        )[: state_ref.shape[2]]
        state_ref[0, c] = state
        total = state if c == 0 else state + keep(seg_ref, c - 1) * total
    cut_up(total, seg_ref, piece_ref)


def key_kernel(
    chunks, window_ref, key_ref, value_ref, map_ref, seg_col_ref, seg_row_ref,
    feat_high_ref, feat_low_ref, feat_t_ref, value_t_ref, value_pair_ref, kind_ref,
):
    reach = window_ref[pl.program_id(0)]
    upper, lower = softmaxes(mm(key_ref[...], map_ref[0]), 1)
    features = jnp.concatenate([upper, lower], 1)
    high, low = halves(features)
    feat_high_ref[0] = high
    feat_low_ref[0] = low
    values = value_ref[...]
    value_pair_ref[0] = jnp.concatenate([values, values], 1)
    wide_values = values.astype(F32)
    for c in range(chunks):
        rows = slice(CHUNK * c, CHUNK * c + NEAR)
        turned_high, turned_low = halves(features[rows].T)
        feat_t_ref[0, c] = jnp.concatenate([turned_high, turned_low], 1)
        value_t = wide_values[rows].T.astype(BF16)
        value_t_ref[0, c] = jnp.concatenate([value_t, value_t], 1)
        near_row = lax.broadcasted_iota(jnp.int32, (NEAR, 128), 0)
        token = lax.broadcasted_iota(jnp.int32, (NEAR, 128), 1) % CHUNK
        distance = CHUNK + token - near_row
        same_doc = seg_col_ref[rows] == seg_row_ref[c, :, :128]
        inside = distance < reach
        own = near_row >= CHUNK
        kind = jnp.where(inside, jnp.where(own, OWN_NEAR, RIM_NEAR), jnp.where(own, OWN_FAR, 0.0))
        kind_ref[0, c] = jnp.where(same_doc & (distance >= 0), kind, 0.0).astype(BF16)


def kinds(kind_ref, c):
    kind = kind_ref[0, c].astype(F32)
    return jnp.concatenate([kind] * (LANES // 128), 1)


def signed(kind, linear):
    return jnp.where(kind == OWN_FAR, linear, jnp.where(kind == RIM_NEAR, -linear, 0.0))


def cut_up(total, seg_ref, piece_ref):
    share = piece_ref.shape[1] - 8
    width = total.shape[1]
    end = seg_ref[seg_ref.shape[0] - 1].astype(F32)
    extra = jnp.where(
        lax.broadcasted_iota(jnp.int32, (8, width), 0) == 0, total[128:136], end
    )
    for i in range(piece_ref.shape[0]):
        piece_ref[i, :share] = total[share * i : share * (i + 1)]
        piece_ref[i, share:] = extra


def whole_state(piece):
    share = piece.shape[1] - 8
    state = side(0, share, piece)
    norm = jnp.broadcast_to(piece[0, share : share + 1], (8, piece.shape[2]))
    return jnp.concatenate([state, norm], 0)


def scan_kernel(count, backward, piece_ref, out_ref):
    mark = piece_ref.shape[1] - 7
    total = jnp.zeros(piece_ref.shape[1:], F32)
    for position in range(count - 1, -1, -1) if backward else range(count):
        out_ref[position] = total
        piece = piece_ref[position]
        former = piece_ref[max(position - 1, 0), mark : mark + 1]
        total = piece + jnp.where(piece[mark : mark + 1] == former, total, 0.0)


def place_diagonal(blocks, diag_ref):
    for i, block in enumerate(blocks):
        diag_ref[i * CHUNK : (i + 1) * CHUNK, i * 128 : (i + 1) * 128] = block


def local_kernel(
    chunks, q0_ref, q1_ref, q2_ref, q3_ref, m0_ref, m1_ref, m2_ref, m3_ref, key_ref, high_ref,
    low_ref, value_t_ref, kind_ref, *refs,
):
    numer_ref, denom_ref, qf_high_ref, qf_low_ref, diag_ref = refs[-5:]

    @pl.when(pl.program_id(0) + pl.program_id(1) == 0)
    def _():
        diag_ref[...] = jnp.zeros_like(diag_ref)

    q_refs = (q0_ref, q1_ref, q2_ref, q3_ref)
    maps = jnp.concatenate([ref[0] for ref in (m0_ref, m1_ref, m2_ref, m3_ref)], 0)
    maps = maps.astype(F32).T.astype(BF16)
    every = range(chunks)
    near = [slice(CHUNK * c, CHUNK * c + NEAR) for c in every]
    blocks = [[ref[CHUNK * c : CHUNK * (c + 1)] for ref in q_refs] for c in every]
    for c in every:
        place_diagonal(blocks[c], diag_ref.at[c])
    logits = [mm_nt(maps, diag_ref[c]) for c in every]
    scores = [mm_nt(key_ref[near[c]], jnp.concatenate(blocks[c], 0)) for c in every]
    cuts = [halves(jnp.concatenate(softmaxes(logits[c], 0), 0)) for c in every]
    both = [
        mm(jnp.concatenate([high_ref[0, near[c]], low_ref[0, near[c]]], 0), cuts[c][0])
        for c in every
    ]
    third = [mm(high_ref[0, near[c]], cuts[c][1]) for c in every]
    for c in every:
        qf_high_ref[0, c], qf_low_ref[0, c] = cuts[c]
        kind = kinds(kind_ref, c)
        score = jnp.where(kind >= OWN_NEAR, scores[c] * 128 ** (-0.5), MASKED)
        weights = jnp.exp(score - jnp.max(score, axis=0, keepdims=True))
        linear = both[c][:NEAR] + both[c][NEAR:] + third[c]
        weights = weights + signed(kind, linear)
        denom_ref[0, c] = jnp.sum(weights, axis=0, keepdims=True)
        numer_ref[0, c] = mm(value_t_ref[0, c], jnp.concatenate(halves(weights), 0))


def enter_states(chunks, seg_ref, first_ref, state_ref, rows_ref, columns_ref, norm_ref):
    state = whole_state(first_ref)
    for c in range(chunks):
        if c > 0:
            state = state_ref[0, c - 1] + keep(seg_ref, c - 1) * state
        high, low = halves(jnp.concatenate([state, state[128:]], 0))
        rows_ref[c] = jnp.concatenate([high, low], 0)
        columns_ref[0, c] = jnp.concatenate(halves(state[:128].T), 1)
        norm_ref[0, c] = state[128:]


def output_kernel(
    chunks, seg_ref, t0_ref, t1_ref, t2_ref, t3_ref, numer_ref, denom_ref, qf_high_ref, qf_low_ref,
    first_ref, state_ref, value_pair_ref, kind_ref, seg_row_ref, right_ref,
    grad_denom_ref, key_grad_ref, state_grad_ref, piece_ref, columns_ref, norm_ref, rows_ref,
):
    begins = pl.program_id(1) + pl.program_id(2) == 0
    ends = (pl.program_id(1) == 1) & (pl.program_id(2) == pl.num_programs(2) - 1)

    @pl.when(begins)
    def _():
        enter_states(chunks, seg_ref, first_ref, state_ref, rows_ref, columns_ref, norm_ref)

    t_refs = (t0_ref, t1_ref, t2_ref, t3_ref)
    padded = rows_ref.shape[1] // 2
    every = range(chunks)
    carried = [
        jnp.where(seg_row_ref[c] == seg_ref[c * CHUNK + CHUNK - 1], 1.0, 0.0).astype(F32)
        for c in every
    ]
    both = [mm(rows_ref[c], qf_high_ref[0, c]) for c in every]
    third = [mm(rows_ref[c, :padded], qf_low_ref[0, c]) for c in every]
    cuts, grad_denoms = [], []
    for c in every:
        carry = (both[c][:padded] + both[c][padded:] + third[c]) * carried[c]
        inverse = 1.0 / (denom_ref[0, c] + carry[128:129])
        outputs = (numer_ref[0, c] + carry[:128]) * inverse
        targets = jnp.concatenate([ref[CHUNK * c : CHUNK * (c + 1)] for ref in t_refs], 0)
        residual = outputs - targets.astype(F32).T
        grad_denom = -jnp.sum(residual * outputs, axis=0, keepdims=True) * inverse
        grad_denom_ref[0, c] = grad_denom * carried[c]
        grad_denoms.append(grad_denom)
        cuts.append(halves(residual * inverse))
    linear = [
        mm(value_pair_ref[0, CHUNK * c : CHUNK * c + NEAR], jnp.concatenate(cuts[c], 0))
        for c in every
    ]
    left_high, left_low = [], []
    for c in every:
        linear_high, linear_low = halves(
            signed(kinds(kind_ref, c), linear[c] + grad_denoms[c])
        )
        mask = carried[c].astype(BF16)
        grad_high, grad_low = cuts[c][0] * mask, cuts[c][1] * mask
        right_ref[0, c] = jnp.concatenate([linear_high, linear_low, grad_high, grad_low], 0)
        denom_high, denom_low = halves(
            jnp.broadcast_to(grad_denoms[c] * carried[c], (16, LANES))
        )
        left_high.append(jnp.concatenate([linear_high, grad_high, denom_high], 0))
        left_low.append(jnp.concatenate([linear_low, grad_low, denom_low], 0))
    both = [
        mm_nt(jnp.concatenate([left_high[c], left_low[c]], 0), qf_high_ref[0, c]) for c in every
    ]
    third = [mm_nt(left_high[c], qf_low_ref[0, c]) for c in every]
    rows = NEAR + padded
    results = [both[c][:rows] + both[c][rows:] + third[c] for c in every]

    @pl.when(begins)
    def _():
        for c in range(chunks):
            key_grad_ref[0, c] = results[c][:NEAR]
            state_grad_ref[0, c] = results[c][NEAR : NEAR + 136]

    @pl.when(jnp.logical_not(begins))
    def _():
        for c in range(chunks):
            key_grad_ref[0, c] += results[c][:NEAR]
            state_grad_ref[0, c] += results[c][NEAR : NEAR + 136]

    @pl.when(ends)
    def _():
        total = state_grad_ref[0, chunks - 1]
        for c in range(chunks - 2, -1, -1):
            total = state_grad_ref[0, c] + keep(seg_ref, c) * total
        cut_up(total, seg_ref, piece_ref)


def query_kernel(
    chunks, core_ref, q0_ref, q1_ref, q2_ref, q3_ref, right_ref, grad_denom_ref, qf_high_ref,
    qf_low_ref, feat_t_ref, columns_ref, norm_ref, *refs,
):
    mine_ref, theirs_ref, diag_ref, left_ref, spread_ref = refs[-5:]

    @pl.when(pl.program_id(0) + pl.program_id(1) == 0)
    def _():
        diag_ref[...] = jnp.zeros_like(diag_ref)

    @pl.when(pl.program_id(1) == 0)
    def _():
        for c in range(chunks):
            feat_high, feat_low = feat_t_ref[0, c, :, :NEAR], feat_t_ref[0, c, :, NEAR:]
            state_high, state_low = columns_ref[0, c, :, :128], columns_ref[0, c, :, 128:]
            left_ref[c] = jnp.concatenate(
                [feat_high, feat_high, state_high, state_high, feat_low, state_low], 1
            )
            norm = jnp.broadcast_to(norm_ref[0, c, :1], (128, norm_ref.shape[3]))
            spread_ref[c] = norm.T

    q_refs = (q0_ref, q1_ref, q2_ref, q3_ref)
    every = range(chunks)
    for c in every:
        place_diagonal([ref[CHUNK * c : CHUNK * (c + 1)] for ref in q_refs], diag_ref.at[c])
    feature_grads = []
    for c in every:
        stack = right_ref[0, c]
        right = jnp.concatenate([stack, stack[:NEAR], stack[2 * NEAR : 2 * NEAR + 128]], 0)
        feature_grads.append(mm(left_ref[c], right))
    cuts = []
    for c in every:
        norm = jnp.concatenate([spread_ref[c]] * (LANES // 128), 1)
        feature_grad = feature_grads[c] + norm * grad_denom_ref[0, c]
        high, low = qf_high_ref[0, c], qf_low_ref[0, c]
        upper = high[:128].astype(F32) + low[:128].astype(F32)
        lower = high[128:].astype(F32) + low[128:].astype(F32)
        cuts.append(
            halves(softmax_grads(upper, lower, feature_grad[:128], feature_grad[128:], 0))
        )
    both = [mm(jnp.concatenate(cuts[c], 0), diag_ref[c]) for c in every]
    total = sum(x[:128] + x[128:] for x in both)

    for core, own in enumerate(((mine_ref, theirs_ref), (theirs_ref, mine_ref))):

        @pl.when(core_ref[0] == core)
        def _(own=own):
            for i in range(QUAD):
                own[i % 2][i // 2] = total[:, i * 128 : (i + 1) * 128]


def tail_kernel(
    chunks, seg_ref, key_ref, value_ref, map_ref, seg_col_ref, later_ref, state_grad_ref,
    key_grad_ref, out_ref,
):
    logits = mm(key_ref[...], map_ref[0])
    upper, lower = softmaxes(logits, 1)
    values = value_ref[...]
    pieces = [key_grad_ref[0, 0, :CHUNK]]
    leaving = whole_state(later_ref)
    states = []
    for c in range(chunks - 1, -1, -1):
        states.append(leaving)
        leaving = state_grad_ref[0, c] + keep(seg_ref, c) * leaving
    states = states[::-1]
    for c in range(chunks):
        own = slice(CHUNK * (c + 1), CHUNK * (c + 2))
        grads = key_grad_ref[0, c, CHUNK:]
        if c + 1 < chunks:
            grads = grads + key_grad_ref[0, c + 1, :CHUNK]
        tail = jnp.where(seg_col_ref[own] == seg_ref[CHUNK * (c + 2) - 1], 1.0, 0.0).astype(F32)
        entry_high, entry_low = halves(states[c][:128])
        through = mm(
            jnp.concatenate([values[own], values[own]], 1),
            jnp.concatenate([entry_high, entry_low], 0),
        )
        pieces.append(grads + tail * (through + states[c][128:129]))
    grads = jnp.concatenate(pieces, 0)
    logit_grad = softmax_grads(upper, lower, grads[:, :128], grads[:, 128:], 1)
    turned = key_ref[...].astype(F32).T.astype(BF16)
    out_ref[0] = mm(
        jnp.concatenate([turned, turned], 1), jnp.concatenate(halves(logit_grad), 0)
    )


def call(
    kernel, name, microseconds, grid, in_specs, out_specs, out_shape, args, scalars=0, scratch=(),
    aliases=None,
):
    return pl.pallas_call(
        kernel,
        grid_spec=pltpu.PrefetchScalarGridSpec(
            num_scalar_prefetch=scalars,
            grid=grid,
            in_specs=in_specs,
            out_specs=out_specs,
            scratch_shapes=scratch,
        ),
        out_shape=out_shape,
        compiler_params=pltpu.CompilerParams(vmem_limit_bytes=VMEM_LIMIT),
        cost_estimate=pl.CostEstimate(
            flops=int(microseconds * 1e9), bytes_accessed=int(microseconds * 3e6), transcendentals=0
        ),
        input_output_aliases=aliases or {},
        name=name,
    )(*args)


def exchange(pieces, axis):
    return lax.all_to_all(pieces, axis, 0, 0, tiled=True)


def on_device(queries, keys, values, targets, segments, window, query_feature_projection, key_map):
    head_count, head_dim, map_width = query_feature_projection.shape
    groups = key_map.shape[0]
    tok_rows = queries.shape[1]
    near_rows = tok_rows + CHUNK
    chunks = tok_rows // CHUNK
    features = 2 * map_width
    quads = head_count // groups // QUAD // 2
    ctx, dp = lax.axis_size("ctx"), lax.axis_size("dp")
    me = lax.axis_index("ctx")
    state_rows = head_dim + 8
    sds = jax.ShapeDtypeStruct

    seg_row = segments[0]
    seg_rows = jnp.tile(seg_row.reshape(chunks, 1, CHUNK), (1, 1, QUAD))
    query_rows, target_rows = queries[0], targets[0]
    group_spec = lambda *shape: pl.BlockSpec((1,) + shape, lambda g, *_: (g,) + (0,) * len(shape))
    whole = lambda shape: pl.BlockSpec(shape, lambda *_: (0,) * len(shape))
    column = lambda rows: pl.BlockSpec((rows, head_dim), lambda g, *_: (0, g))
    per_group = ctx // groups
    piece_shape = (ctx, head_dim // per_group + 8, features)
    piece_spec = pl.BlockSpec((per_group,) + piece_shape[1:], lambda g, *_: (g, 0, 0))

    chunk_state, block_pieces = call(
        functools.partial(block_kernel, chunks), "block", 4, (groups,),
        [
            column(tok_rows), column(tok_rows), group_spec(head_dim, map_width),
            whole((chunks, 1, LANES)),
        ],
        [group_spec(chunks, state_rows, features), piece_spec],
        [sds((groups, chunks, state_rows, features), F32), sds(piece_shape, F32)],
        (seg_row, keys[0], values[0], key_map, seg_rows),
        scalars=1,
    )

    def across(pieces, backward, first, second):
        received, aside = lax.optimization_barrier((exchange(pieces, "ctx"), first()))
        summed = call(
            functools.partial(scan_kernel, ctx, backward), "scan", 2, (1,), [whole(piece_shape)],
            whole(piece_shape), sds(piece_shape, F32), (received,),
        )
        summed, aside = lax.optimization_barrier((summed, aside))
        return lax.optimization_barrier((exchange(summed, "ctx"), second(aside)))

    rim = jnp.concatenate([keys[0, -CHUNK:], values[0, -CHUNK:]], 1)
    rim_seg = jnp.broadcast_to(seg_row[-CHUNK:].astype(BF16)[:, None], (CHUNK, 128))
    rim = lax.ppermute(
        jnp.concatenate([rim, rim_seg], 1), "ctx", [(i, i + 1) for i in range(ctx - 1)]
    )
    width = keys.shape[2]
    near_keys = jnp.concatenate([rim[:, :width], keys[0]], 0)
    near_values = jnp.concatenate([rim[:, width : 2 * width], values[0]], 0)
    rim_segments = jnp.where(me > 0, rim[:, 2 * width].astype(jnp.int32), -1)
    near_segments = jnp.concatenate([rim_segments, seg_row], 0)
    seg_col = near_segments[:, None]
    feat_high, feat_low, feat_t, value_t, value_pair, kind = call(
        functools.partial(key_kernel, chunks), "keys", 5, (groups,),
        [
            column(near_rows), column(near_rows), group_spec(head_dim, map_width),
            whole((near_rows, 1)), whole((chunks, 1, LANES)),
        ],
        [
            group_spec(near_rows, features), group_spec(near_rows, features),
            group_spec(chunks, features, 2 * NEAR), group_spec(chunks, head_dim, 2 * NEAR),
            group_spec(near_rows, 2 * head_dim), group_spec(chunks, NEAR, 128),
        ],
        [
            sds((groups, near_rows, features), BF16), sds((groups, near_rows, features), BF16),
            sds((groups, chunks, features, 2 * NEAR), BF16),
            sds((groups, chunks, head_dim, 2 * NEAR), BF16),
            sds((groups, near_rows, 2 * head_dim), BF16),
            sds((groups, chunks, NEAR, 128), BF16),
        ],
        (window, near_keys, near_values, key_map, seg_col, seg_rows),
        scalars=1,
    )

    half_steps = groups * quads
    steps = 2 * half_steps
    grid = (groups, quads)
    spot = lambda g, q: g * quads + q

    def step_spec(half, *shape):
        return pl.BlockSpec(
            (1,) + shape, lambda g, q, *_: (half * half_steps + spot(g, q),) + (0,) * len(shape)
        )

    def head_specs(half):
        return [
            pl.BlockSpec(
                (tok_rows, head_dim), lambda g, q, *_, i=i: (0, (spot(g, q) * QUAD + i) * 2 + half)
            )
            for i in range(QUAD)
        ]

    def local(half, so_far):
        map_specs = [
            pl.BlockSpec(
                (1, head_dim, map_width),
                lambda g, q, *_, i=i: ((spot(g, q) * QUAD + i) * 2 + half, 0, 0),
            )
            for i in range(QUAD)
        ]
        step = functools.partial(step_spec, half)
        return call(
            functools.partial(local_kernel, chunks), "local", 15, grid,
            head_specs(half) + map_specs
            + [
                column(near_rows), group_spec(near_rows, features),
                group_spec(near_rows, features), group_spec(chunks, head_dim, 2 * NEAR),
                group_spec(chunks, NEAR, 128),
            ]
            + [pl.BlockSpec(memory_space=pl.ANY)] * len(so_far),
            [
                step(chunks, head_dim, LANES), step(chunks, 1, LANES),
                step(chunks, features, LANES), step(chunks, features, LANES),
            ],
            [
                sds((steps, chunks, head_dim, LANES), F32), sds((steps, chunks, 1, LANES), F32),
                sds((steps, chunks, features, LANES), BF16),
                sds((steps, chunks, features, LANES), BF16),
            ],
            (
                *([query_rows] * QUAD), *([query_feature_projection] * QUAD), near_keys, feat_high,
                feat_low, value_t, kind, *so_far,
            ),
            scratch=[pltpu.VMEM((chunks, LANES, QUAD * head_dim), BF16)],
            aliases={13 + i: i for i in range(len(so_far))},
        )

    entering, forward = across(
        block_pieces, False, lambda: local(0, ()), lambda so_far: local(1, so_far)
    )

    every_step = lambda *shape: pl.BlockSpec(
        (1,) + shape, lambda g, h, q, *_: (h * half_steps + spot(g, q),) + (0,) * len(shape)
    )
    right, grad_denom, key_grad, state_grad, grad_pieces, columns, norms = call(
        functools.partial(output_kernel, chunks), "outputs", 45, (groups, 2, quads),
        [
            pl.BlockSpec(
                (tok_rows, head_dim),
                lambda g, h, q, *_, i=i: (0, (spot(g, q) * QUAD + i) * 2 + h),
            )
            for i in range(QUAD)
        ]
        + [
            every_step(chunks, head_dim, LANES), every_step(chunks, 1, LANES),
            every_step(chunks, features, LANES), every_step(chunks, features, LANES),
            piece_spec, group_spec(chunks, state_rows, features),
            group_spec(near_rows, 2 * head_dim), group_spec(chunks, NEAR, 128),
            whole((chunks, 1, LANES)),
        ],
        [
            every_step(chunks, 4 * NEAR, LANES), every_step(chunks, 1, LANES),
            group_spec(chunks, NEAR, features), group_spec(chunks, state_rows, features),
            piece_spec, group_spec(chunks, features, 2 * head_dim), group_spec(chunks, 8, features),
        ],
        [
            sds((steps, chunks, 4 * NEAR, LANES), BF16), sds((steps, chunks, 1, LANES), F32),
            sds((groups, chunks, NEAR, features), F32),
            sds((groups, chunks, state_rows, features), F32), sds(piece_shape, F32),
            sds((groups, chunks, features, 2 * head_dim), BF16),
            sds((groups, chunks, 8, features), F32),
        ],
        (
            near_segments, *([target_rows] * QUAD), *forward, entering, chunk_state, value_pair,
            kind, seg_rows,
        ),
        scalars=1,
        scratch=[pltpu.VMEM((chunks, 2 * (state_rows + 8), features), BF16)],
    )

    core = lax.rem(me, 2)
    partner = [(i, i ^ 1) for i in range(ctx)]

    def query(half, right, start, count, so_far=()):
        part = pl.BlockSpec(
            (QUAD // 2, map_width, head_dim), lambda g, q, *_: (spot(g + start, q), 0, 0)
        )
        shape = sds((head_count // 4, map_width, head_dim), F32)
        from_start = lambda spec: pl.BlockSpec(
            spec.block_shape, lambda g, q, *_: spec.index_map(g + start, q)
        )
        step = functools.partial(step_spec, half)
        specs = head_specs(half) + [
            step(chunks, 4 * NEAR, LANES), step(chunks, 1, LANES), step(chunks, features, LANES),
            step(chunks, features, LANES), group_spec(chunks, features, 2 * NEAR),
            group_spec(chunks, features, 2 * head_dim), group_spec(chunks, 8, features),
        ]
        return call(
            functools.partial(query_kernel, chunks), "queries", 10 * count // groups,
            (count, quads),
            [from_start(spec) for spec in specs]
            + [pl.BlockSpec(memory_space=pl.ANY)] * len(so_far),
            [part, part], [shape, shape],
            (
                core[None], *([query_rows] * QUAD), right, grad_denom, *forward[2:], feat_t,
                columns, norms, *so_far,
            ),
            scalars=1,
            scratch=[
                pltpu.VMEM((chunks, LANES, QUAD * head_dim), BF16),
                pltpu.VMEM((chunks, features, 6 * 128), BF16),
                pltpu.VMEM((chunks, features, 128), F32),
            ],
            aliases={12 + i: i for i in range(len(so_far))},
        )

    same_core = [[i for i in range(ctx) if i % 2 == k] for k in range(2)]

    def around(axis, value):
        if axis == "dp":
            routes = [[(i, (i + s) % dp) for i in range(dp)] for s in range(1, RING)]
        else:
            stride = 2 if axis == "z" else 2 * RING
            at = lambda i, s: i + ((i // stride + s) % RING - i // stride % RING) * stride
            routes = [[(i, at(i, s)) for i in range(ctx)] for s in range(1, RING)]
            axis = "ctx"
        one, two, three = (lax.ppermute(value, axis, route) for route in routes)
        return (value + two) + (one + three)

    def over_cores(mine, theirs):
        return mine + lax.ppermute(theirs, "ctx", partner)

    def over_chips(pieces):
        received = lax.all_to_all(pieces, "ctx", 0, 0, tiled=True, axis_index_groups=same_core)
        return jnp.sum(received.reshape(ctx // 2, -1, map_width, head_dim), axis=0)

    def second_half(done):
        first, right = lax.optimization_barrier((over_cores(*done[0]), done[1]))
        return first, query(1, right, 0, groups)

    later, (first, second) = across(
        grad_pieces, True, lambda: (query(0, right, 0, groups), right), second_half
    )
    second = over_cores(*second)
    later, first, second = lax.optimization_barrier((later, first, second))

    key_grad = call(
        functools.partial(tail_kernel, chunks), "tail", 5, (groups,),
        [
            column(near_rows), column(near_rows), group_spec(head_dim, map_width),
            whole((near_rows, 1)), piece_spec, group_spec(chunks, state_rows, features),
            group_spec(chunks, NEAR, features),
        ],
        group_spec(head_dim, map_width), sds((groups, head_dim, map_width), F32),
        (
            near_segments, near_keys, near_values, key_map, seg_col, later, state_grad, key_grad,
        ),
        scalars=1,
    )

    key_halves = key_grad.reshape(2, -1, map_width)
    key_mine = lax.dynamic_index_in_dim(key_halves, core, 0, False)
    key_theirs = lax.dynamic_index_in_dim(key_halves, 1 - core, 0, False)
    key_mine = over_cores(key_mine, key_theirs)
    key_mine = around("dp", around("x", around("z", key_mine)))
    key_theirs = lax.ppermute(key_mine, "ctx", partner)
    full_key = jnp.concatenate(
        [jnp.where(core == 0, key_mine, key_theirs), jnp.where(core == 0, key_theirs, key_mine)], 0
    )
    full_query = around("dp", over_chips(jnp.stack([first, second], 1)))
    return (full_query.transpose(0, 2, 1), full_key.reshape(groups, head_dim, map_width))


def solution(mesh):
    return jax.shard_map(
        on_device,
        mesh=mesh,
        in_specs=(
            P("dp", "ctx", None),
            P("dp", "ctx", None),
            P("dp", "ctx", None),
            P("dp", "ctx", None),
            P("dp", "ctx"),
            P(),
            P(),
            P(),
        ),
        out_specs=(P("ctx", None, None), P()),
        check_vma=False,
    )
```

```python
import functools
import jax
import jax.numpy as jnp
from jax import lax
from jax.experimental import pallas as pl
from jax.experimental.pallas import tpu as pltpu
from jax.sharding import PartitionSpec as P

CHUNK = 64
QUAD = 4
LANES = QUAD * CHUNK
NEAR = 2 * CHUNK
MASKED = -1e30
OWN_FAR, OWN_NEAR, RIM_NEAR = 1.0, 2.0, 3.0
F32 = jnp.float32
BF16 = jnp.bfloat16
RING = 4
VMEM_LIMIT = 60 * 1024 * 1024


def halves(x):
    high = x.astype(BF16)
    return high, (x - high.astype(F32)).astype(BF16)


def mm(a, b):
    return jnp.dot(a, b, preferred_element_type=F32)


def mm_nt(a, b):
    return lax.dot_general(a, b, (((1,), (1,)), ((), ())), preferred_element_type=F32)


def softmaxes(logits, axis):
    upper = jnp.exp(logits - jnp.max(logits, axis=axis, keepdims=True))
    lower = jnp.exp(jnp.min(logits, axis=axis, keepdims=True) - logits)
    return (
        upper * (1.0 / jnp.sum(upper, axis=axis, keepdims=True)),
        lower * (1.0 / jnp.sum(lower, axis=axis, keepdims=True)),
    )


def softmax_grads(upper, lower, grad_upper, grad_lower, axis):
    return upper * (
        grad_upper - jnp.sum(upper * grad_upper, axis=axis, keepdims=True)
    ) - lower * (grad_lower - jnp.sum(lower * grad_lower, axis=axis, keepdims=True))


def keep(seg_ref, chunk):
    same = seg_ref[CHUNK * (chunk + 1) - 1] == seg_ref[CHUNK * (chunk + 2) - 1]
    return jnp.where(same, 1.0, 0.0).astype(F32)


def side(first, count, piece):
    return piece[:, first : first + count].reshape(-1, piece.shape[2])


def block_kernel(
    chunks, seg_ref, key_ref, value_ref, map_ref, seg_row_ref, state_ref, piece_ref
):
    upper, lower = softmaxes(mm(key_ref[...], map_ref[0]), 1)
    high, low = halves(jnp.concatenate([upper, lower], 1))
    values = value_ref[...].astype(F32)
    total = None
    for c in range(chunks):
        own = slice(CHUNK * c, CHUNK * (c + 1))
        tail = seg_row_ref[c, :, :CHUNK] == seg_ref[CHUNK * (c + 1) - 1]
        turned = jnp.concatenate([values[own].T, jnp.ones((16, CHUNK), F32)], 0)
        turned = jnp.where(tail, turned, 0.0).astype(BF16)
        state = mm(
            jnp.concatenate([turned, turned], 1), jnp.concatenate([high[own], low[own]], 0)
        )[: state_ref.shape[2]]
        state_ref[0, c] = state
        total = state if c == 0 else state + keep(seg_ref, c - 1) * total
    cut_up(total, seg_ref, piece_ref)


def key_kernel(
    chunks, window_ref, key_ref, value_ref, map_ref, seg_col_ref, seg_row_ref,
    feat_high_ref, feat_low_ref, feat_t_ref, value_t_ref, value_pair_ref, kind_ref,
):
    reach = window_ref[pl.program_id(0)]
    upper, lower = softmaxes(mm(key_ref[...], map_ref[0]), 1)
    features = jnp.concatenate([upper, lower], 1)
    high, low = halves(features)
    feat_high_ref[0] = high
    feat_low_ref[0] = low
    values = value_ref[...]
    value_pair_ref[0] = jnp.concatenate([values, values], 1)
    wide_values = values.astype(F32)
    for c in range(chunks):
        rows = slice(CHUNK * c, CHUNK * c + NEAR)
        turned_high, turned_low = halves(features[rows].T)
        feat_t_ref[0, c] = jnp.concatenate([turned_high, turned_low], 1)
        value_t = wide_values[rows].T.astype(BF16)
        value_t_ref[0, c] = jnp.concatenate([value_t, value_t], 1)
        near_row = lax.broadcasted_iota(jnp.int32, (NEAR, 128), 0)
        token = lax.broadcasted_iota(jnp.int32, (NEAR, 128), 1) % CHUNK
        distance = CHUNK + token - near_row
        same_doc = seg_col_ref[rows] == seg_row_ref[c, :, :128]
        inside = distance < reach
        own = near_row >= CHUNK
        kind = jnp.where(inside, jnp.where(own, OWN_NEAR, RIM_NEAR), jnp.where(own, OWN_FAR, 0.0))
        kind_ref[0, c] = jnp.where(same_doc & (distance >= 0), kind, 0.0).astype(BF16)


def kinds(kind_ref, c):
    kind = kind_ref[0, c].astype(F32)
    return jnp.concatenate([kind] * (LANES // 128), 1)


def signed(kind, linear):
    return jnp.where(kind == OWN_FAR, linear, jnp.where(kind == RIM_NEAR, -linear, 0.0))


def cut_up(total, seg_ref, piece_ref):
    share = piece_ref.shape[1] - 8
    width = total.shape[1]
    end = seg_ref[seg_ref.shape[0] - 1].astype(F32)
    extra = jnp.where(
        lax.broadcasted_iota(jnp.int32, (8, width), 0) == 0, total[128:136], end
    )
    for i in range(piece_ref.shape[0]):
        piece_ref[i, :share] = total[share * i : share * (i + 1)]
        piece_ref[i, share:] = extra


def whole_state(piece):
    share = piece.shape[1] - 8
    state = side(0, share, piece)
    norm = jnp.broadcast_to(piece[0, share : share + 1], (8, piece.shape[2]))
    return jnp.concatenate([state, norm], 0)


def scan_kernel(count, backward, piece_ref, out_ref):
    mark = piece_ref.shape[1] - 7
    total = jnp.zeros(piece_ref.shape[1:], F32)
    for position in range(count - 1, -1, -1) if backward else range(count):
        out_ref[position] = total
        piece = piece_ref[position]
        former = piece_ref[max(position - 1, 0), mark : mark + 1]
        total = piece + jnp.where(piece[mark : mark + 1] == former, total, 0.0)


def place_diagonal(blocks, diag_ref):
    for i, block in enumerate(blocks):
        diag_ref[i * CHUNK : (i + 1) * CHUNK, i * 128 : (i + 1) * 128] = block


def local_kernel(
    chunks, q0_ref, q1_ref, q2_ref, q3_ref, m0_ref, m1_ref, m2_ref, m3_ref, key_ref, high_ref,
    low_ref, value_t_ref, kind_ref, *refs,
):
    numer_ref, denom_ref, qf_high_ref, qf_low_ref, diag_ref = refs[-5:]

    @pl.when(pl.program_id(0) + pl.program_id(1) == 0)
    def _():
        diag_ref[...] = jnp.zeros_like(diag_ref)

    q_refs = (q0_ref, q1_ref, q2_ref, q3_ref)
    maps = jnp.concatenate([ref[0] for ref in (m0_ref, m1_ref, m2_ref, m3_ref)], 0)
    maps = maps.astype(F32).T.astype(BF16)
    every = range(chunks)
    near = [slice(CHUNK * c, CHUNK * c + NEAR) for c in every]
    blocks = [[ref[CHUNK * c : CHUNK * (c + 1)] for ref in q_refs] for c in every]
    for c in every:
        place_diagonal(blocks[c], diag_ref.at[c])
    logits = [mm_nt(maps, diag_ref[c]) for c in every]
    scores = [mm_nt(key_ref[near[c]], jnp.concatenate(blocks[c], 0)) for c in every]
    cuts = [halves(jnp.concatenate(softmaxes(logits[c], 0), 0)) for c in every]
    both = [
        mm(jnp.concatenate([high_ref[0, near[c]], low_ref[0, near[c]]], 0), cuts[c][0])
        for c in every
    ]
    third = [mm(high_ref[0, near[c]], cuts[c][1]) for c in every]
    for c in every:
        qf_high_ref[0, c], qf_low_ref[0, c] = cuts[c]
        kind = kinds(kind_ref, c)
        score = jnp.where(kind >= OWN_NEAR, scores[c] * 128 ** (-0.5), MASKED)
        weights = jnp.exp(score - jnp.max(score, axis=0, keepdims=True))
        linear = both[c][:NEAR] + both[c][NEAR:] + third[c]
        weights = weights + signed(kind, linear)
        denom_ref[0, c] = jnp.sum(weights, axis=0, keepdims=True)
        numer_ref[0, c] = mm(value_t_ref[0, c], jnp.concatenate(halves(weights), 0))


def enter_states(chunks, seg_ref, first_ref, state_ref, rows_ref, columns_ref, norm_ref):
    state = whole_state(first_ref)
    for c in range(chunks):
        if c > 0:
            state = state_ref[0, c - 1] + keep(seg_ref, c - 1) * state
        high, low = halves(jnp.concatenate([state, state[128:]], 0))
        rows_ref[c] = jnp.concatenate([high, low], 0)
        columns_ref[0, c] = jnp.concatenate(halves(state[:128].T), 1)
        norm_ref[0, c] = state[128:]


def output_kernel(
    chunks, seg_ref, t0_ref, t1_ref, t2_ref, t3_ref, numer_ref, denom_ref, qf_high_ref, qf_low_ref,
    first_ref, state_ref, value_pair_ref, kind_ref, seg_row_ref, right_ref,
    grad_denom_ref, key_grad_ref, state_grad_ref, piece_ref, columns_ref, norm_ref, rows_ref,
):
    begins = pl.program_id(1) + pl.program_id(2) == 0
    ends = (pl.program_id(1) == 1) & (pl.program_id(2) == pl.num_programs(2) - 1)

    @pl.when(begins)
    def _():
        enter_states(chunks, seg_ref, first_ref, state_ref, rows_ref, columns_ref, norm_ref)

    t_refs = (t0_ref, t1_ref, t2_ref, t3_ref)
    padded = rows_ref.shape[1] // 2
    every = range(chunks)
    carried = [
        jnp.where(seg_row_ref[c] == seg_ref[c * CHUNK + CHUNK - 1], 1.0, 0.0).astype(F32)
        for c in every
    ]
    both = [mm(rows_ref[c], qf_high_ref[0, c]) for c in every]
    third = [mm(rows_ref[c, :padded], qf_low_ref[0, c]) for c in every]
    cuts, grad_denoms = [], []
    for c in every:
        carry = (both[c][:padded] + both[c][padded:] + third[c]) * carried[c]
        inverse = 1.0 / (denom_ref[0, c] + carry[128:129])
        outputs = (numer_ref[0, c] + carry[:128]) * inverse
        targets = jnp.concatenate([ref[CHUNK * c : CHUNK * (c + 1)] for ref in t_refs], 0)
        residual = outputs - targets.astype(F32).T
        grad_denom = -jnp.sum(residual * outputs, axis=0, keepdims=True) * inverse
        grad_denom_ref[0, c] = grad_denom * carried[c]
        grad_denoms.append(grad_denom)
        cuts.append(halves(residual * inverse))
    linear = [
        mm(value_pair_ref[0, CHUNK * c : CHUNK * c + NEAR], jnp.concatenate(cuts[c], 0))
        for c in every
    ]
    left_high, left_low = [], []
    for c in every:
        linear_high, linear_low = halves(
            signed(kinds(kind_ref, c), linear[c] + grad_denoms[c])
        )
        mask = carried[c].astype(BF16)
        grad_high, grad_low = cuts[c][0] * mask, cuts[c][1] * mask
        right_ref[0, c] = jnp.concatenate([linear_high, linear_low, grad_high, grad_low], 0)
        denom_high, denom_low = halves(
            jnp.broadcast_to(grad_denoms[c] * carried[c], (16, LANES))
        )
        left_high.append(jnp.concatenate([linear_high, grad_high, denom_high], 0))
        left_low.append(jnp.concatenate([linear_low, grad_low, denom_low], 0))
    both = [
        mm_nt(jnp.concatenate([left_high[c], left_low[c]], 0), qf_high_ref[0, c]) for c in every
    ]
    third = [mm_nt(left_high[c], qf_low_ref[0, c]) for c in every]
    rows = NEAR + padded
    results = [both[c][:rows] + both[c][rows:] + third[c] for c in every]

    @pl.when(begins)
    def _():
        for c in range(chunks):
            key_grad_ref[0, c] = results[c][:NEAR]
            state_grad_ref[0, c] = results[c][NEAR : NEAR + 136]

    @pl.when(jnp.logical_not(begins))
    def _():
        for c in range(chunks):
            key_grad_ref[0, c] += results[c][:NEAR]
            state_grad_ref[0, c] += results[c][NEAR : NEAR + 136]

    @pl.when(ends)
    def _():
        total = state_grad_ref[0, chunks - 1]
        for c in range(chunks - 2, -1, -1):
            total = state_grad_ref[0, c] + keep(seg_ref, c) * total
        cut_up(total, seg_ref, piece_ref)


def query_kernel(
    chunks, core_ref, q0_ref, q1_ref, q2_ref, q3_ref, right_ref, grad_denom_ref, qf_high_ref,
    qf_low_ref, feat_t_ref, columns_ref, norm_ref, *refs,
):
    mine_ref, theirs_ref, diag_ref, left_ref, spread_ref = refs[-5:]

    @pl.when(pl.program_id(0) + pl.program_id(1) == 0)
    def _():
        diag_ref[...] = jnp.zeros_like(diag_ref)

    @pl.when(pl.program_id(1) == 0)
    def _():
        for c in range(chunks):
            feat_high, feat_low = feat_t_ref[0, c, :, :NEAR], feat_t_ref[0, c, :, NEAR:]
            state_high, state_low = columns_ref[0, c, :, :128], columns_ref[0, c, :, 128:]
            left_ref[c] = jnp.concatenate(
                [feat_high, feat_high, state_high, state_high, feat_low, state_low], 1
            )
            norm = jnp.broadcast_to(norm_ref[0, c, :1], (128, norm_ref.shape[3]))
            spread_ref[c] = norm.T

    q_refs = (q0_ref, q1_ref, q2_ref, q3_ref)
    every = range(chunks)
    for c in every:
        place_diagonal([ref[CHUNK * c : CHUNK * (c + 1)] for ref in q_refs], diag_ref.at[c])
    feature_grads = []
    for c in every:
        stack = right_ref[0, c]
        right = jnp.concatenate([stack, stack[:NEAR], stack[2 * NEAR : 2 * NEAR + 128]], 0)
        feature_grads.append(mm(left_ref[c], right))
    cuts = []
    for c in every:
        norm = jnp.concatenate([spread_ref[c]] * (LANES // 128), 1)
        feature_grad = feature_grads[c] + norm * grad_denom_ref[0, c]
        high, low = qf_high_ref[0, c], qf_low_ref[0, c]
        upper = high[:128].astype(F32) + low[:128].astype(F32)
        lower = high[128:].astype(F32) + low[128:].astype(F32)
        cuts.append(
            halves(softmax_grads(upper, lower, feature_grad[:128], feature_grad[128:], 0))
        )
    both = [mm(jnp.concatenate(cuts[c], 0), diag_ref[c]) for c in every]
    total = sum(x[:128] + x[128:] for x in both)

    for core, own in enumerate(((mine_ref, theirs_ref), (theirs_ref, mine_ref))):

        @pl.when(core_ref[0] == core)
        def _(own=own):
            for i in range(QUAD):
                own[i % 2][i // 2, 0] = total[:, i * 128 : (i + 1) * 128]


def tail_kernel(
    chunks, seg_ref, key_ref, value_ref, map_ref, seg_col_ref, later_ref, state_grad_ref,
    key_grad_ref, out_ref,
):
    logits = mm(key_ref[...], map_ref[0])
    upper, lower = softmaxes(logits, 1)
    values = value_ref[...]
    pieces = [key_grad_ref[0, 0, :CHUNK]]
    leaving = whole_state(later_ref)
    states = []
    for c in range(chunks - 1, -1, -1):
        states.append(leaving)
        leaving = state_grad_ref[0, c] + keep(seg_ref, c) * leaving
    states = states[::-1]
    for c in range(chunks):
        own = slice(CHUNK * (c + 1), CHUNK * (c + 2))
        grads = key_grad_ref[0, c, CHUNK:]
        if c + 1 < chunks:
            grads = grads + key_grad_ref[0, c + 1, :CHUNK]
        tail = jnp.where(seg_col_ref[own] == seg_ref[CHUNK * (c + 2) - 1], 1.0, 0.0).astype(F32)
        entry_high, entry_low = halves(states[c][:128])
        through = mm(
            jnp.concatenate([values[own], values[own]], 1),
            jnp.concatenate([entry_high, entry_low], 0),
        )
        pieces.append(grads + tail * (through + states[c][128:129]))
    grads = jnp.concatenate(pieces, 0)
    logit_grad = softmax_grads(upper, lower, grads[:, :128], grads[:, 128:], 1)
    turned = key_ref[...].astype(F32).T.astype(BF16)
    out_ref[0] = mm(
        jnp.concatenate([turned, turned], 1), jnp.concatenate(halves(logit_grad), 0)
    )


def call(
    kernel, name, microseconds, grid, in_specs, out_specs, out_shape, args, scalars=0, scratch=(),
    aliases=None,
):
    return pl.pallas_call(
        kernel,
        grid_spec=pltpu.PrefetchScalarGridSpec(
            num_scalar_prefetch=scalars,
            grid=grid,
            in_specs=in_specs,
            out_specs=out_specs,
            scratch_shapes=scratch,
        ),
        out_shape=out_shape,
        compiler_params=pltpu.CompilerParams(vmem_limit_bytes=VMEM_LIMIT),
        cost_estimate=pl.CostEstimate(
            flops=int(microseconds * 1e9), bytes_accessed=int(microseconds * 3e6), transcendentals=0
        ),
        input_output_aliases=aliases or {},
        name=name,
    )(*args)


def exchange(pieces, axis):
    return lax.all_to_all(pieces, axis, 0, 0, tiled=True)


def on_device(queries, keys, values, targets, segments, window, query_feature_projection, key_map):
    head_count, head_dim, map_width = query_feature_projection.shape
    groups = key_map.shape[0]
    tok_rows = queries.shape[1]
    near_rows = tok_rows + CHUNK
    chunks = tok_rows // CHUNK
    features = 2 * map_width
    quads = head_count // groups // QUAD // 2
    ctx, dp = lax.axis_size("ctx"), lax.axis_size("dp")
    me = lax.axis_index("ctx")
    state_rows = head_dim + 8
    sds = jax.ShapeDtypeStruct

    seg_row = segments[0]
    seg_rows = jnp.tile(seg_row.reshape(chunks, 1, CHUNK), (1, 1, QUAD))
    query_rows, target_rows = queries[0], targets[0]
    group_spec = lambda *shape: pl.BlockSpec((1,) + shape, lambda g, *_: (g,) + (0,) * len(shape))
    whole = lambda shape: pl.BlockSpec(shape, lambda *_: (0,) * len(shape))
    column = lambda rows: pl.BlockSpec((rows, head_dim), lambda g, *_: (0, g))
    per_group = ctx // groups
    piece_shape = (ctx, head_dim // per_group + 8, features)
    piece_spec = pl.BlockSpec((per_group,) + piece_shape[1:], lambda g, *_: (g, 0, 0))

    chunk_state, block_pieces = call(
        functools.partial(block_kernel, chunks), "block", 4, (groups,),
        [
            column(tok_rows), column(tok_rows), group_spec(head_dim, map_width),
            whole((chunks, 1, LANES)),
        ],
        [group_spec(chunks, state_rows, features), piece_spec],
        [sds((groups, chunks, state_rows, features), F32), sds(piece_shape, F32)],
        (seg_row, keys[0], values[0], key_map, seg_rows),
        scalars=1,
    )

    def across(pieces, backward, first, second):
        received, aside = lax.optimization_barrier((exchange(pieces, "ctx"), first()))
        summed = call(
            functools.partial(scan_kernel, ctx, backward), "scan", 2, (1,), [whole(piece_shape)],
            whole(piece_shape), sds(piece_shape, F32), (received,),
        )
        summed, aside = lax.optimization_barrier((summed, aside))
        done, free = second(aside)
        return *lax.optimization_barrier((exchange(summed, "ctx"), done)), free

    block_pieces, row_keys, row_values = lax.optimization_barrier(
        (block_pieces, keys[0], values[0])
    )
    rim = jnp.concatenate([row_keys[-CHUNK:], row_values[-CHUNK:]], 1)
    rim_seg = jnp.broadcast_to(seg_row[-CHUNK:].astype(BF16)[:, None], (CHUNK, 128))
    rim = lax.ppermute(
        jnp.concatenate([rim, rim_seg], 1), "ctx", [(i, i + 1) for i in range(ctx - 1)]
    )
    width = keys.shape[2]
    near_keys = jnp.concatenate([rim[:, :width], row_keys], 0)
    near_values = jnp.concatenate([rim[:, width : 2 * width], row_values], 0)
    rim_segments = jnp.where(me > 0, rim[:, 2 * width].astype(jnp.int32), -1)
    near_segments = jnp.concatenate([rim_segments, seg_row], 0)
    seg_col = near_segments[:, None]
    feat_high, feat_low, feat_t, value_t, value_pair, kind = call(
        functools.partial(key_kernel, chunks), "keys", 5, (groups,),
        [
            column(near_rows), column(near_rows), group_spec(head_dim, map_width),
            whole((near_rows, 1)), whole((chunks, 1, LANES)),
        ],
        [
            group_spec(near_rows, features), group_spec(near_rows, features),
            group_spec(chunks, features, 2 * NEAR), group_spec(chunks, head_dim, 2 * NEAR),
            group_spec(near_rows, 2 * head_dim), group_spec(chunks, NEAR, 128),
        ],
        [
            sds((groups, near_rows, features), BF16), sds((groups, near_rows, features), BF16),
            sds((groups, chunks, features, 2 * NEAR), BF16),
            sds((groups, chunks, head_dim, 2 * NEAR), BF16),
            sds((groups, near_rows, 2 * head_dim), BF16),
            sds((groups, chunks, NEAR, 128), BF16),
        ],
        (window, near_keys, near_values, key_map, seg_col, seg_rows),
        scalars=1,
    )

    half_steps = groups * quads
    steps = 2 * half_steps
    grid = (groups, quads)
    spot = lambda g, q: g * quads + q

    def step_spec(half, *shape):
        return pl.BlockSpec(
            (1,) + shape, lambda g, q, *_: (half * half_steps + spot(g, q),) + (0,) * len(shape)
        )

    def head_specs(half):
        return [
            pl.BlockSpec(
                (tok_rows, head_dim), lambda g, q, *_, i=i: (0, (spot(g, q) * QUAD + i) * 2 + half)
            )
            for i in range(QUAD)
        ]

    def local(half, so_far):
        map_specs = [
            pl.BlockSpec(
                (1, head_dim, map_width),
                lambda g, q, *_, i=i: ((spot(g, q) * QUAD + i) * 2 + half, 0, 0),
            )
            for i in range(QUAD)
        ]
        step = functools.partial(step_spec, half)
        return call(
            functools.partial(local_kernel, chunks), "local", 15, grid,
            head_specs(half) + map_specs
            + [
                column(near_rows), group_spec(near_rows, features),
                group_spec(near_rows, features), group_spec(chunks, head_dim, 2 * NEAR),
                group_spec(chunks, NEAR, 128),
            ]
            + [pl.BlockSpec(memory_space=pl.ANY)] * len(so_far),
            [
                step(chunks, head_dim, LANES), step(chunks, 1, LANES),
                step(chunks, features, LANES), step(chunks, features, LANES),
            ],
            [
                sds((steps, chunks, head_dim, LANES), F32), sds((steps, chunks, 1, LANES), F32),
                sds((steps, chunks, features, LANES), BF16),
                sds((steps, chunks, features, LANES), BF16),
            ],
            (
                *([query_rows] * QUAD), *([query_feature_projection] * QUAD), near_keys, feat_high,
                feat_low, value_t, kind, *so_far,
            ),
            scratch=[pltpu.VMEM((chunks, LANES, QUAD * head_dim), BF16)],
            aliases={13 + i: i for i in range(len(so_far))},
        )

    entering, forward, _ = across(
        block_pieces, False, lambda: local(0, ()), lambda so_far: (local(1, so_far), None)
    )

    every_step = lambda *shape: pl.BlockSpec(
        (1,) + shape, lambda g, h, q, *_: (h * half_steps + spot(g, q),) + (0,) * len(shape)
    )
    right, grad_denom, key_grad, state_grad, grad_pieces, columns, norms = call(
        functools.partial(output_kernel, chunks), "outputs", 45, (groups, 2, quads),
        [
            pl.BlockSpec(
                (tok_rows, head_dim),
                lambda g, h, q, *_, i=i: (0, (spot(g, q) * QUAD + i) * 2 + h),
            )
            for i in range(QUAD)
        ]
        + [
            every_step(chunks, head_dim, LANES), every_step(chunks, 1, LANES),
            every_step(chunks, features, LANES), every_step(chunks, features, LANES),
            piece_spec, group_spec(chunks, state_rows, features),
            group_spec(near_rows, 2 * head_dim), group_spec(chunks, NEAR, 128),
            whole((chunks, 1, LANES)),
        ],
        [
            every_step(chunks, 4 * NEAR, LANES), every_step(chunks, 1, LANES),
            group_spec(chunks, NEAR, features), group_spec(chunks, state_rows, features),
            piece_spec, group_spec(chunks, features, 2 * head_dim), group_spec(chunks, 8, features),
        ],
        [
            sds((steps, chunks, 4 * NEAR, LANES), BF16), sds((steps, chunks, 1, LANES), F32),
            sds((groups, chunks, NEAR, features), F32),
            sds((groups, chunks, state_rows, features), F32), sds(piece_shape, F32),
            sds((groups, chunks, features, 2 * head_dim), BF16),
            sds((groups, chunks, 8, features), F32),
        ],
        (
            near_segments, *([target_rows] * QUAD), *forward, entering, chunk_state, value_pair,
            kind, seg_rows,
        ),
        scalars=1,
        scratch=[pltpu.VMEM((chunks, 2 * (state_rows + 8), features), BF16)],
    )

    core = lax.rem(me, 2)
    partner = [(i, i ^ 1) for i in range(ctx)]

    def query(half, right, start, count, so_far=()):
        part = pl.BlockSpec(
            (QUAD // 2, 1, map_width, head_dim), lambda g, q, *_: (q, g + start, 0, 0)
        )
        shape = sds((RING, RING, map_width, head_dim), F32)
        from_start = lambda spec: pl.BlockSpec(
            spec.block_shape, lambda g, q, *_: spec.index_map(g + start, q)
        )
        step = functools.partial(step_spec, half)
        specs = head_specs(half) + [
            step(chunks, 4 * NEAR, LANES), step(chunks, 1, LANES), step(chunks, features, LANES),
            step(chunks, features, LANES), group_spec(chunks, features, 2 * NEAR),
            group_spec(chunks, features, 2 * head_dim), group_spec(chunks, 8, features),
        ]
        return call(
            functools.partial(query_kernel, chunks), "queries", 10 * count // groups,
            (count, quads),
            [from_start(spec) for spec in specs]
            + [pl.BlockSpec(memory_space=pl.ANY)] * len(so_far),
            [part, part], [shape, shape],
            (
                core[None], *([query_rows] * QUAD), right, grad_denom, *forward[2:], feat_t,
                columns, norms, *so_far,
            ),
            scalars=1,
            scratch=[
                pltpu.VMEM((chunks, LANES, QUAD * head_dim), BF16),
                pltpu.VMEM((chunks, features, 6 * 128), BF16),
                pltpu.VMEM((chunks, features, 128), F32),
            ],
            aliases={12 + i: i for i in range(len(so_far))},
        )

    place = {"z": me // 2 % RING, "x": me // (2 * RING)}

    def routes(axis):
        if axis == "dp":
            return [[(i, (i + s) % dp) for i in range(dp)] for s in range(1, RING)]
        stride = 2 if axis == "z" else 2 * RING
        at = lambda i, s: i + ((i // stride + s) % RING - i // stride % RING) * stride
        return [[(i, at(i, s)) for i in range(ctx)] for s in range(1, RING)]

    def add_up(own, one, two, three):
        return (own + two) + (one + three)

    def around(axis, value):
        name = axis if axis == "dp" else "ctx"
        return add_up(value, *(lax.ppermute(value, name, route) for route in routes(axis)))

    def slice_around(axis, dim, *values):
        own, *others = [
            sum(
                lax.dynamic_index_in_dim(value, lax.rem(place[axis] + s, RING), dim, False)
                for value in values
            )
            for s in range(RING)
        ]
        return add_up(
            own, *(lax.ppermute(part, "ctx", route) for part, route in zip(others, routes(axis)))
        )

    def over_chip(mine, theirs):
        return mine, lax.ppermute(theirs, "ctx", partner)

    def second_half(done):
        first, right = lax.optimization_barrier((over_chip(*done[0]), done[1]))
        return query(1, right, 0, groups), slice_around("z", 0, *first)

    later, second, first = across(
        grad_pieces, True, lambda: (query(0, right, 0, groups), right), second_half
    )

    key_grad = call(
        functools.partial(tail_kernel, chunks), "tail", 5, (groups,),
        [
            column(near_rows), column(near_rows), group_spec(head_dim, map_width),
            whole((near_rows, 1)), piece_spec, group_spec(chunks, state_rows, features),
            group_spec(chunks, NEAR, features),
        ],
        group_spec(head_dim, map_width), sds((groups, head_dim, map_width), F32),
        (
            near_segments, near_keys, near_values, key_map, seg_col, later, state_grad, key_grad,
        ),
        scalars=1,
    )

    key_grad, first = lax.optimization_barrier((key_grad, first))
    key_halves = key_grad.reshape(2, -1, map_width)
    key_mine = lax.dynamic_index_in_dim(key_halves, core, 0, False)
    key_theirs = lax.dynamic_index_in_dim(key_halves, 1 - core, 0, False)
    key_mine, key_theirs = over_chip(key_mine, key_theirs)
    second = over_chip(*second)
    key_sum, second = lax.optimization_barrier((key_mine + key_theirs, second))
    key_sum = around("x", around("dp", around("z", key_sum)))
    second = slice_around("z", 0, slice_around("x", 1, *second))
    first = slice_around("x", 0, first)
    both = around("dp", jnp.stack([first, second], 0))
    key_theirs = lax.ppermute(key_sum, "ctx", partner)
    full_key = jnp.concatenate(
        [jnp.where(core == 0, key_sum, key_theirs), jnp.where(core == 0, key_theirs, key_sum)], 0
    )
    return (both.transpose(0, 2, 1), full_key.reshape(groups, head_dim, map_width))


def solution(mesh):
    return jax.shard_map(
        on_device,
        mesh=mesh,
        in_specs=(
            P("dp", "ctx", None),
            P("dp", "ctx", None),
            P("dp", "ctx", None),
            P("dp", "ctx", None),
            P("dp", "ctx"),
            P(),
            P(),
            P(),
        ),
        out_specs=(P("ctx", None, None), P()),
        check_vma=False,
    )
```

```python
import functools
import jax
import jax.numpy as jnp
from jax import lax
from jax.experimental import pallas as pl
from jax.experimental.pallas import tpu as pltpu
from jax.sharding import PartitionSpec as P

CHUNK = 64
QUAD = 4
LANES = QUAD * CHUNK
NEAR = 2 * CHUNK
MASKED = -1e30
OWN_FAR, OWN_NEAR, RIM_NEAR = 1.0, 2.0, 3.0
F32 = jnp.float32
BF16 = jnp.bfloat16
RING = 4
VMEM_LIMIT = 60 * 1024 * 1024


def halves(x):
    high = x.astype(BF16)
    return high, (x - high.astype(F32)).astype(BF16)


def mm(a, b):
    return jnp.dot(a, b, preferred_element_type=F32)


def mm_nt(a, b):
    return lax.dot_general(a, b, (((1,), (1,)), ((), ())), preferred_element_type=F32)


def softmaxes(logits, axis):
    upper = jnp.exp(logits - jnp.max(logits, axis=axis, keepdims=True))
    lower = jnp.exp(jnp.min(logits, axis=axis, keepdims=True) - logits)
    return (
        upper * (1.0 / jnp.sum(upper, axis=axis, keepdims=True)),
        lower * (1.0 / jnp.sum(lower, axis=axis, keepdims=True)),
    )


def softmax_grads(upper, lower, grad_upper, grad_lower, axis):
    return upper * (
        grad_upper - jnp.sum(upper * grad_upper, axis=axis, keepdims=True)
    ) - lower * (grad_lower - jnp.sum(lower * grad_lower, axis=axis, keepdims=True))


def keep(seg_ref, chunk):
    same = seg_ref[CHUNK * (chunk + 1) - 1] == seg_ref[CHUNK * (chunk + 2) - 1]
    return jnp.where(same, 1.0, 0.0).astype(F32)


def side(first, count, piece):
    return piece[:, first : first + count].reshape(-1, piece.shape[2])


def block_kernel(
    chunks, seg_ref, key_ref, value_ref, map_ref, seg_row_ref, state_ref, piece_ref
):
    upper, lower = softmaxes(mm(key_ref[...], map_ref[0]), 1)
    high, low = halves(jnp.concatenate([upper, lower], 1))
    values = value_ref[...].astype(F32)
    total = None
    for c in range(chunks):
        own = slice(CHUNK * c, CHUNK * (c + 1))
        tail = seg_row_ref[c, :, :CHUNK] == seg_ref[CHUNK * (c + 1) - 1]
        turned = jnp.concatenate([values[own].T, jnp.ones((16, CHUNK), F32)], 0)
        turned = jnp.where(tail, turned, 0.0).astype(BF16)
        state = mm(
            jnp.concatenate([turned, turned], 1), jnp.concatenate([high[own], low[own]], 0)
        )[: state_ref.shape[2]]
        state_ref[0, c] = state
        total = state if c == 0 else state + keep(seg_ref, c - 1) * total
    cut_up(total, seg_ref, piece_ref)


def key_kernel(
    chunks, window_ref, key_ref, value_ref, map_ref, seg_col_ref, seg_row_ref,
    feat_high_ref, feat_low_ref, feat_t_ref, value_t_ref, value_pair_ref, kind_ref,
):
    reach = window_ref[pl.program_id(0)]
    upper, lower = softmaxes(mm(key_ref[...], map_ref[0]), 1)
    features = jnp.concatenate([upper, lower], 1)
    high, low = halves(features)
    feat_high_ref[0] = high
    feat_low_ref[0] = low
    values = value_ref[...]
    value_pair_ref[0] = jnp.concatenate([values, values], 1)
    wide_values = values.astype(F32)
    for c in range(chunks):
        rows = slice(CHUNK * c, CHUNK * c + NEAR)
        turned_high, turned_low = halves(features[rows].T)
        feat_t_ref[0, c] = jnp.concatenate([turned_high, turned_low], 1)
        value_t = wide_values[rows].T.astype(BF16)
        value_t_ref[0, c] = jnp.concatenate([value_t, value_t], 1)
        near_row = lax.broadcasted_iota(jnp.int32, (NEAR, 128), 0)
        token = lax.broadcasted_iota(jnp.int32, (NEAR, 128), 1) % CHUNK
        distance = CHUNK + token - near_row
        same_doc = seg_col_ref[rows] == seg_row_ref[c, :, :128]
        inside = distance < reach
        own = near_row >= CHUNK
        kind = jnp.where(inside, jnp.where(own, OWN_NEAR, RIM_NEAR), jnp.where(own, OWN_FAR, 0.0))
        kind_ref[0, c] = jnp.where(same_doc & (distance >= 0), kind, 0.0).astype(BF16)


def kinds(kind_ref, c):
    kind = kind_ref[0, c].astype(F32)
    return jnp.concatenate([kind] * (LANES // 128), 1)


def signed(kind, linear):
    return jnp.where(kind == OWN_FAR, linear, jnp.where(kind == RIM_NEAR, -linear, 0.0))


def cut_up(total, seg_ref, piece_ref):
    share = piece_ref.shape[1] - 8
    width = total.shape[1]
    end = seg_ref[seg_ref.shape[0] - 1].astype(F32)
    extra = jnp.where(
        lax.broadcasted_iota(jnp.int32, (8, width), 0) == 0, total[128:136], end
    )
    for i in range(piece_ref.shape[0]):
        piece_ref[i, :share] = total[share * i : share * (i + 1)]
        piece_ref[i, share:] = extra


def whole_state(piece):
    share = piece.shape[1] - 8
    state = side(0, share, piece)
    norm = jnp.broadcast_to(piece[0, share : share + 1], (8, piece.shape[2]))
    return jnp.concatenate([state, norm], 0)


def scan_kernel(count, backward, piece_ref, out_ref):
    mark = piece_ref.shape[1] - 7
    total = jnp.zeros(piece_ref.shape[1:], F32)
    for position in range(count - 1, -1, -1) if backward else range(count):
        out_ref[position] = total
        piece = piece_ref[position]
        former = piece_ref[max(position - 1, 0), mark : mark + 1]
        total = piece + jnp.where(piece[mark : mark + 1] == former, total, 0.0)


def place_diagonal(blocks, diag_ref):
    for i, block in enumerate(blocks):
        diag_ref[i * CHUNK : (i + 1) * CHUNK, i * 128 : (i + 1) * 128] = block


def local_kernel(
    chunks, q0_ref, q1_ref, q2_ref, q3_ref, m0_ref, m1_ref, m2_ref, m3_ref, key_ref, high_ref,
    low_ref, value_t_ref, kind_ref, *refs,
):
    numer_ref, denom_ref, qf_high_ref, qf_low_ref, diag_ref = refs[-5:]

    @pl.when(pl.program_id(0) + pl.program_id(1) == 0)
    def _():
        diag_ref[...] = jnp.zeros_like(diag_ref)

    q_refs = (q0_ref, q1_ref, q2_ref, q3_ref)
    maps = jnp.concatenate([ref[0] for ref in (m0_ref, m1_ref, m2_ref, m3_ref)], 0)
    maps = maps.astype(F32).T.astype(BF16)
    every = range(chunks)
    near = [slice(CHUNK * c, CHUNK * c + NEAR) for c in every]
    blocks = [[ref[CHUNK * c : CHUNK * (c + 1)] for ref in q_refs] for c in every]
    for c in every:
        place_diagonal(blocks[c], diag_ref.at[c])
    logits = [mm_nt(maps, diag_ref[c]) for c in every]
    scores = [mm_nt(key_ref[near[c]], jnp.concatenate(blocks[c], 0)) for c in every]
    cuts = [halves(jnp.concatenate(softmaxes(logits[c], 0), 0)) for c in every]
    both = [
        mm(jnp.concatenate([high_ref[0, near[c]], low_ref[0, near[c]]], 0), cuts[c][0])
        for c in every
    ]
    third = [mm(high_ref[0, near[c]], cuts[c][1]) for c in every]
    for c in every:
        qf_high_ref[0, c], qf_low_ref[0, c] = cuts[c]
        kind = kinds(kind_ref, c)
        score = jnp.where(kind >= OWN_NEAR, scores[c] * 128 ** (-0.5), MASKED)
        weights = jnp.exp(score - jnp.max(score, axis=0, keepdims=True))
        linear = both[c][:NEAR] + both[c][NEAR:] + third[c]
        weights = weights + signed(kind, linear)
        denom_ref[0, c] = jnp.sum(weights, axis=0, keepdims=True)
        numer_ref[0, c] = mm(value_t_ref[0, c], jnp.concatenate(halves(weights), 0))


def enter_states(chunks, seg_ref, first_ref, state_ref, rows_ref, columns_ref, norm_ref):
    state = whole_state(first_ref)
    for c in range(chunks):
        if c > 0:
            state = state_ref[0, c - 1] + keep(seg_ref, c - 1) * state
        high, low = halves(jnp.concatenate([state, state[128:]], 0))
        rows_ref[c] = jnp.concatenate([high, low], 0)
        columns_ref[0, c] = jnp.concatenate(halves(state[:128].T), 1)
        norm_ref[0, c] = state[128:]


def output_kernel(
    chunks, seg_ref, t0_ref, t1_ref, t2_ref, t3_ref, numer_ref, denom_ref, qf_high_ref, qf_low_ref,
    first_ref, state_ref, value_pair_ref, kind_ref, seg_row_ref, right_ref,
    grad_denom_ref, key_grad_ref, state_grad_ref, piece_ref, columns_ref, norm_ref, rows_ref,
):
    begins = pl.program_id(1) + pl.program_id(2) == 0
    ends = (pl.program_id(1) == 1) & (pl.program_id(2) == pl.num_programs(2) - 1)

    @pl.when(begins)
    def _():
        enter_states(chunks, seg_ref, first_ref, state_ref, rows_ref, columns_ref, norm_ref)

    t_refs = (t0_ref, t1_ref, t2_ref, t3_ref)
    padded = rows_ref.shape[1] // 2
    every = range(chunks)
    carried = [
        jnp.where(seg_row_ref[c] == seg_ref[c * CHUNK + CHUNK - 1], 1.0, 0.0).astype(F32)
        for c in every
    ]
    both = [mm(rows_ref[c], qf_high_ref[0, c]) for c in every]
    third = [mm(rows_ref[c, :padded], qf_low_ref[0, c]) for c in every]
    cuts, grad_denoms = [], []
    for c in every:
        carry = (both[c][:padded] + both[c][padded:] + third[c]) * carried[c]
        inverse = 1.0 / (denom_ref[0, c] + carry[128:129])
        outputs = (numer_ref[0, c] + carry[:128]) * inverse
        targets = jnp.concatenate([ref[CHUNK * c : CHUNK * (c + 1)] for ref in t_refs], 0)
        residual = outputs - targets.astype(F32).T
        grad_denom = -jnp.sum(residual * outputs, axis=0, keepdims=True) * inverse
        grad_denom_ref[0, c] = grad_denom * carried[c]
        grad_denoms.append(grad_denom)
        cuts.append(halves(residual * inverse))
    linear = [
        mm(value_pair_ref[0, CHUNK * c : CHUNK * c + NEAR], jnp.concatenate(cuts[c], 0))
        for c in every
    ]
    left_high, left_low = [], []
    for c in every:
        linear_high, linear_low = halves(
            signed(kinds(kind_ref, c), linear[c] + grad_denoms[c])
        )
        mask = carried[c].astype(BF16)
        grad_high, grad_low = cuts[c][0] * mask, cuts[c][1] * mask
        right_ref[0, c] = jnp.concatenate([linear_high, linear_low, grad_high, grad_low], 0)
        denom_high, denom_low = halves(
            jnp.broadcast_to(grad_denoms[c] * carried[c], (16, LANES))
        )
        left_high.append(jnp.concatenate([linear_high, grad_high, denom_high], 0))
        left_low.append(jnp.concatenate([linear_low, grad_low, denom_low], 0))
    both = [
        mm_nt(jnp.concatenate([left_high[c], left_low[c]], 0), qf_high_ref[0, c]) for c in every
    ]
    third = [mm_nt(left_high[c], qf_low_ref[0, c]) for c in every]
    rows = NEAR + padded
    results = [both[c][:rows] + both[c][rows:] + third[c] for c in every]

    @pl.when(begins)
    def _():
        for c in range(chunks):
            key_grad_ref[0, c] = results[c][:NEAR]
            state_grad_ref[0, c] = results[c][NEAR : NEAR + 136]

    @pl.when(jnp.logical_not(begins))
    def _():
        for c in range(chunks):
            key_grad_ref[0, c] += results[c][:NEAR]
            state_grad_ref[0, c] += results[c][NEAR : NEAR + 136]

    @pl.when(ends)
    def _():
        total = state_grad_ref[0, chunks - 1]
        for c in range(chunks - 2, -1, -1):
            total = state_grad_ref[0, c] + keep(seg_ref, c) * total
        cut_up(total, seg_ref, piece_ref)


def query_kernel(
    chunks, core_ref, q0_ref, q1_ref, q2_ref, q3_ref, right_ref, grad_denom_ref, qf_high_ref,
    qf_low_ref, feat_t_ref, columns_ref, norm_ref, *refs,
):
    mine_ref, theirs_ref, diag_ref, left_ref, spread_ref = refs[-5:]

    @pl.when(pl.program_id(0) + pl.program_id(1) == 0)
    def _():
        diag_ref[...] = jnp.zeros_like(diag_ref)

    @pl.when(pl.program_id(1) == 0)
    def _():
        for c in range(chunks):
            feat_high, feat_low = feat_t_ref[0, c, :, :NEAR], feat_t_ref[0, c, :, NEAR:]
            state_high, state_low = columns_ref[0, c, :, :128], columns_ref[0, c, :, 128:]
            left_ref[c] = jnp.concatenate(
                [feat_high, feat_high, state_high, state_high, feat_low, state_low], 1
            )
            norm = jnp.broadcast_to(norm_ref[0, c, :1], (128, norm_ref.shape[3]))
            spread_ref[c] = norm.T

    q_refs = (q0_ref, q1_ref, q2_ref, q3_ref)
    every = range(chunks)
    for c in every:
        place_diagonal([ref[CHUNK * c : CHUNK * (c + 1)] for ref in q_refs], diag_ref.at[c])
    feature_grads = []
    for c in every:
        stack = right_ref[0, c]
        right = jnp.concatenate([stack, stack[:NEAR], stack[2 * NEAR : 2 * NEAR + 128]], 0)
        feature_grads.append(mm(left_ref[c], right))
    cuts = []
    for c in every:
        norm = jnp.concatenate([spread_ref[c]] * (LANES // 128), 1)
        feature_grad = feature_grads[c] + norm * grad_denom_ref[0, c]
        high, low = qf_high_ref[0, c], qf_low_ref[0, c]
        upper = high[:128].astype(F32) + low[:128].astype(F32)
        lower = high[128:].astype(F32) + low[128:].astype(F32)
        cuts.append(
            halves(softmax_grads(upper, lower, feature_grad[:128], feature_grad[128:], 0))
        )
    both = [mm(jnp.concatenate(cuts[c], 0), diag_ref[c]) for c in every]
    total = sum(x[:128] + x[128:] for x in both)

    for core, own in enumerate(((mine_ref, theirs_ref), (theirs_ref, mine_ref))):

        @pl.when(core_ref[0] == core)
        def _(own=own):
            for i in range(QUAD):
                own[i % 2][i // 2, 0] = total[:, i * 128 : (i + 1) * 128]


def tail_kernel(
    chunks, seg_ref, key_ref, value_ref, map_ref, seg_col_ref, later_ref, state_grad_ref,
    key_grad_ref, out_ref,
):
    logits = mm(key_ref[...], map_ref[0])
    upper, lower = softmaxes(logits, 1)
    values = value_ref[...]
    pieces = [key_grad_ref[0, 0, :CHUNK]]
    leaving = whole_state(later_ref)
    states = []
    for c in range(chunks - 1, -1, -1):
        states.append(leaving)
        leaving = state_grad_ref[0, c] + keep(seg_ref, c) * leaving
    states = states[::-1]
    for c in range(chunks):
        own = slice(CHUNK * (c + 1), CHUNK * (c + 2))
        grads = key_grad_ref[0, c, CHUNK:]
        if c + 1 < chunks:
            grads = grads + key_grad_ref[0, c + 1, :CHUNK]
        tail = jnp.where(seg_col_ref[own] == seg_ref[CHUNK * (c + 2) - 1], 1.0, 0.0).astype(F32)
        entry_high, entry_low = halves(states[c][:128])
        through = mm(
            jnp.concatenate([values[own], values[own]], 1),
            jnp.concatenate([entry_high, entry_low], 0),
        )
        pieces.append(grads + tail * (through + states[c][128:129]))
    grads = jnp.concatenate(pieces, 0)
    logit_grad = softmax_grads(upper, lower, grads[:, :128], grads[:, 128:], 1)
    turned = key_ref[...].astype(F32).T.astype(BF16)
    out_ref[0] = mm(
        jnp.concatenate([turned, turned], 1), jnp.concatenate(halves(logit_grad), 0)
    )


def call(
    kernel, name, microseconds, grid, in_specs, out_specs, out_shape, args, scalars=0, scratch=(),
    aliases=None,
):
    return pl.pallas_call(
        kernel,
        grid_spec=pltpu.PrefetchScalarGridSpec(
            num_scalar_prefetch=scalars,
            grid=grid,
            in_specs=in_specs,
            out_specs=out_specs,
            scratch_shapes=scratch,
        ),
        out_shape=out_shape,
        compiler_params=pltpu.CompilerParams(vmem_limit_bytes=VMEM_LIMIT),
        cost_estimate=pl.CostEstimate(
            flops=int(microseconds * 1e9), bytes_accessed=int(microseconds * 3e6), transcendentals=0
        ),
        input_output_aliases=aliases or {},
        name=name,
    )(*args)


def exchange(pieces, axis):
    return lax.all_to_all(pieces, axis, 0, 0, tiled=True)


def on_device(queries, keys, values, targets, segments, window, query_feature_projection, key_map):
    head_count, head_dim, map_width = query_feature_projection.shape
    groups = key_map.shape[0]
    tok_rows = queries.shape[1]
    near_rows = tok_rows + CHUNK
    chunks = tok_rows // CHUNK
    features = 2 * map_width
    quads = head_count // groups // QUAD // 2
    ctx, dp = lax.axis_size("ctx"), lax.axis_size("dp")
    me = lax.axis_index("ctx")
    state_rows = head_dim + 8
    sds = jax.ShapeDtypeStruct

    seg_row = segments[0]
    seg_rows = jnp.tile(seg_row.reshape(chunks, 1, CHUNK), (1, 1, QUAD))
    query_rows, target_rows = queries[0], targets[0]
    group_spec = lambda *shape: pl.BlockSpec((1,) + shape, lambda g, *_: (g,) + (0,) * len(shape))
    whole = lambda shape: pl.BlockSpec(shape, lambda *_: (0,) * len(shape))
    column = lambda rows: pl.BlockSpec((rows, head_dim), lambda g, *_: (0, g))
    per_group = ctx // groups
    piece_shape = (ctx, head_dim // per_group + 8, features)
    piece_spec = pl.BlockSpec((per_group,) + piece_shape[1:], lambda g, *_: (g, 0, 0))

    chunk_state, block_pieces = call(
        functools.partial(block_kernel, chunks), "block", 4, (groups,),
        [
            column(tok_rows), column(tok_rows), group_spec(head_dim, map_width),
            whole((chunks, 1, LANES)),
        ],
        [group_spec(chunks, state_rows, features), piece_spec],
        [sds((groups, chunks, state_rows, features), F32), sds(piece_shape, F32)],
        (seg_row, keys[0], values[0], key_map, seg_rows),
        scalars=1,
    )

    def across(pieces, backward, first, second):
        received, aside = lax.optimization_barrier((exchange(pieces, "ctx"), first()))
        summed = call(
            functools.partial(scan_kernel, ctx, backward), "scan", 2, (1,), [whole(piece_shape)],
            whole(piece_shape), sds(piece_shape, F32), (received,),
        )
        summed, aside = lax.optimization_barrier((summed, aside))
        done, free = second(aside)
        return *lax.optimization_barrier((exchange(summed, "ctx"), done)), free

    block_pieces, row_keys, row_values = lax.optimization_barrier(
        (block_pieces, keys[0], values[0])
    )
    rim = jnp.concatenate([row_keys[-CHUNK:], row_values[-CHUNK:]], 1)
    rim_seg = jnp.broadcast_to(seg_row[-CHUNK:].astype(BF16)[:, None], (CHUNK, 128))
    rim = lax.ppermute(
        jnp.concatenate([rim, rim_seg], 1), "ctx", [(i, i + 1) for i in range(ctx - 1)]
    )
    width = keys.shape[2]
    near_keys = jnp.concatenate([rim[:, :width], row_keys], 0)
    near_values = jnp.concatenate([rim[:, width : 2 * width], row_values], 0)
    rim_segments = jnp.where(me > 0, rim[:, 2 * width].astype(jnp.int32), -1)
    near_segments = jnp.concatenate([rim_segments, seg_row], 0)
    seg_col = near_segments[:, None]
    feat_high, feat_low, feat_t, value_t, value_pair, kind = call(
        functools.partial(key_kernel, chunks), "keys", 5, (groups,),
        [
            column(near_rows), column(near_rows), group_spec(head_dim, map_width),
            whole((near_rows, 1)), whole((chunks, 1, LANES)),
        ],
        [
            group_spec(near_rows, features), group_spec(near_rows, features),
            group_spec(chunks, features, 2 * NEAR), group_spec(chunks, head_dim, 2 * NEAR),
            group_spec(near_rows, 2 * head_dim), group_spec(chunks, NEAR, 128),
        ],
        [
            sds((groups, near_rows, features), BF16), sds((groups, near_rows, features), BF16),
            sds((groups, chunks, features, 2 * NEAR), BF16),
            sds((groups, chunks, head_dim, 2 * NEAR), BF16),
            sds((groups, near_rows, 2 * head_dim), BF16),
            sds((groups, chunks, NEAR, 128), BF16),
        ],
        (window, near_keys, near_values, key_map, seg_col, seg_rows),
        scalars=1,
    )

    half_steps = groups * quads
    steps = 2 * half_steps
    grid = (groups, quads)
    spot = lambda g, q: g * quads + q

    def step_spec(half, *shape):
        return pl.BlockSpec(
            (1,) + shape, lambda g, q, *_: (half * half_steps + spot(g, q),) + (0,) * len(shape)
        )

    def head_specs(half):
        return [
            pl.BlockSpec(
                (tok_rows, head_dim), lambda g, q, *_, i=i: (0, (spot(g, q) * QUAD + i) * 2 + half)
            )
            for i in range(QUAD)
        ]

    def local(half, so_far):
        map_specs = [
            pl.BlockSpec(
                (1, head_dim, map_width),
                lambda g, q, *_, i=i: ((spot(g, q) * QUAD + i) * 2 + half, 0, 0),
            )
            for i in range(QUAD)
        ]
        step = functools.partial(step_spec, half)
        return call(
            functools.partial(local_kernel, chunks), "local", 15, grid,
            head_specs(half) + map_specs
            + [
                column(near_rows), group_spec(near_rows, features),
                group_spec(near_rows, features), group_spec(chunks, head_dim, 2 * NEAR),
                group_spec(chunks, NEAR, 128),
            ]
            + [pl.BlockSpec(memory_space=pl.ANY)] * len(so_far),
            [
                step(chunks, head_dim, LANES), step(chunks, 1, LANES),
                step(chunks, features, LANES), step(chunks, features, LANES),
            ],
            [
                sds((steps, chunks, head_dim, LANES), F32), sds((steps, chunks, 1, LANES), F32),
                sds((steps, chunks, features, LANES), BF16),
                sds((steps, chunks, features, LANES), BF16),
            ],
            (
                *([query_rows] * QUAD), *([query_feature_projection] * QUAD), near_keys, feat_high,
                feat_low, value_t, kind, *so_far,
            ),
            scratch=[pltpu.VMEM((chunks, LANES, QUAD * head_dim), BF16)],
            aliases={13 + i: i for i in range(len(so_far))},
        )

    entering, forward, _ = across(
        block_pieces, False, lambda: local(0, ()), lambda so_far: (local(1, so_far), None)
    )

    every_step = lambda *shape: pl.BlockSpec(
        (1,) + shape, lambda g, h, q, *_: (h * half_steps + spot(g, q),) + (0,) * len(shape)
    )
    right, grad_denom, key_grad, state_grad, grad_pieces, columns, norms = call(
        functools.partial(output_kernel, chunks), "outputs", 45, (groups, 2, quads),
        [
            pl.BlockSpec(
                (tok_rows, head_dim),
                lambda g, h, q, *_, i=i: (0, (spot(g, q) * QUAD + i) * 2 + h),
            )
            for i in range(QUAD)
        ]
        + [
            every_step(chunks, head_dim, LANES), every_step(chunks, 1, LANES),
            every_step(chunks, features, LANES), every_step(chunks, features, LANES),
            piece_spec, group_spec(chunks, state_rows, features),
            group_spec(near_rows, 2 * head_dim), group_spec(chunks, NEAR, 128),
            whole((chunks, 1, LANES)),
        ],
        [
            every_step(chunks, 4 * NEAR, LANES), every_step(chunks, 1, LANES),
            group_spec(chunks, NEAR, features), group_spec(chunks, state_rows, features),
            piece_spec, group_spec(chunks, features, 2 * head_dim), group_spec(chunks, 8, features),
        ],
        [
            sds((steps, chunks, 4 * NEAR, LANES), BF16), sds((steps, chunks, 1, LANES), F32),
            sds((groups, chunks, NEAR, features), F32),
            sds((groups, chunks, state_rows, features), F32), sds(piece_shape, F32),
            sds((groups, chunks, features, 2 * head_dim), BF16),
            sds((groups, chunks, 8, features), F32),
        ],
        (
            near_segments, *([target_rows] * QUAD), *forward, entering, chunk_state, value_pair,
            kind, seg_rows,
        ),
        scalars=1,
        scratch=[pltpu.VMEM((chunks, 2 * (state_rows + 8), features), BF16)],
    )

    core = lax.rem(me, 2)
    partner = [(i, i ^ 1) for i in range(ctx)]

    def query(half, right, start, count, so_far=()):
        part = pl.BlockSpec(
            (QUAD // 2, 1, map_width, head_dim), lambda g, q, *_: (q, g + start, 0, 0)
        )
        shape = sds((RING, RING, map_width, head_dim), F32)
        from_start = lambda spec: pl.BlockSpec(
            spec.block_shape, lambda g, q, *_: spec.index_map(g + start, q)
        )
        step = functools.partial(step_spec, half)
        specs = head_specs(half) + [
            step(chunks, 4 * NEAR, LANES), step(chunks, 1, LANES), step(chunks, features, LANES),
            step(chunks, features, LANES), group_spec(chunks, features, 2 * NEAR),
            group_spec(chunks, features, 2 * head_dim), group_spec(chunks, 8, features),
        ]
        return call(
            functools.partial(query_kernel, chunks), "queries", 10 * count // groups,
            (count, quads),
            [from_start(spec) for spec in specs]
            + [pl.BlockSpec(memory_space=pl.ANY)] * len(so_far),
            [part, part], [shape, shape],
            (
                core[None], *([query_rows] * QUAD), right, grad_denom, *forward[2:], feat_t,
                columns, norms, *so_far,
            ),
            scalars=1,
            scratch=[
                pltpu.VMEM((chunks, LANES, QUAD * head_dim), BF16),
                pltpu.VMEM((chunks, features, 6 * 128), BF16),
                pltpu.VMEM((chunks, features, 128), F32),
            ],
            aliases={12 + i: i for i in range(len(so_far))},
        )

    place = {"z": me // 2 % RING, "x": me // (2 * RING)}

    def routes(axis):
        if axis == "dp":
            return [[(i, (i + s) % dp) for i in range(dp)] for s in range(1, RING)]
        stride = 2 if axis == "z" else 2 * RING
        at = lambda i, s: i + ((i // stride + s) % RING - i // stride % RING) * stride
        return [[(i, at(i, s)) for i in range(ctx)] for s in range(1, RING)]

    def add_up(own, one, two, three):
        return (own + two) + (one + three)

    def around(axis, value):
        name = axis if axis == "dp" else "ctx"
        return add_up(value, *(lax.ppermute(value, name, route) for route in routes(axis)))

    def slice_around(axis, dim, *values):
        own, *others = [
            sum(
                lax.dynamic_index_in_dim(value, lax.rem(place[axis] + s, RING), dim, False)
                for value in values
            )
            for s in range(RING)
        ]
        return add_up(
            own, *(lax.ppermute(part, "ctx", route) for part, route in zip(others, routes(axis)))
        )

    def over_chip(mine, theirs):
        return mine, lax.ppermute(theirs, "ctx", partner)

    def second_half(done):
        first, right = lax.optimization_barrier((over_chip(*done[0]), done[1]))
        some = query(1, right, 0, groups // 2)
        first, some, right = lax.optimization_barrier(
            (slice_around("z", 0, *first), some, right)
        )
        return query(1, right, groups // 2, groups - groups // 2, some), first

    later, second, first = across(
        grad_pieces, True, lambda: (query(0, right, 0, groups), right), second_half
    )

    key_grad = call(
        functools.partial(tail_kernel, chunks), "tail", 5, (groups,),
        [
            column(near_rows), column(near_rows), group_spec(head_dim, map_width),
            whole((near_rows, 1)), piece_spec, group_spec(chunks, state_rows, features),
            group_spec(chunks, NEAR, features),
        ],
        group_spec(head_dim, map_width), sds((groups, head_dim, map_width), F32),
        (
            near_segments, near_keys, near_values, key_map, seg_col, later, state_grad, key_grad,
        ),
        scalars=1,
    )

    key_grad, first = lax.optimization_barrier((key_grad, first))
    key_halves = key_grad.reshape(2, -1, map_width)
    key_mine = lax.dynamic_index_in_dim(key_halves, core, 0, False)
    key_theirs = lax.dynamic_index_in_dim(key_halves, 1 - core, 0, False)
    key_mine, key_theirs = over_chip(key_mine, key_theirs)
    second = over_chip(*second)
    key_sum, second = lax.optimization_barrier((key_mine + key_theirs, second))
    key_sum = around("z", around("dp", around("x", key_sum)))
    second = slice_around("x", 0, slice_around("z", 0, *second))
    first = slice_around("x", 0, first)
    both = around("dp", jnp.stack([first, second], 0))
    key_theirs = lax.ppermute(key_sum, "ctx", partner)
    full_key = jnp.concatenate(
        [jnp.where(core == 0, key_sum, key_theirs), jnp.where(core == 0, key_theirs, key_sum)], 0
    )
    return (both.transpose(0, 2, 1), full_key.reshape(groups, head_dim, map_width))


def solution(mesh):
    return jax.shard_map(
        on_device,
        mesh=mesh,
        in_specs=(
            P("dp", "ctx", None),
            P("dp", "ctx", None),
            P("dp", "ctx", None),
            P("dp", "ctx", None),
            P("dp", "ctx"),
            P(),
            P(),
            P(),
        ),
        out_specs=(P("ctx", None, None), P()),
        check_vma=False,
    )
```

```python
import functools
import jax
import jax.numpy as jnp
from jax import lax
from jax.experimental import pallas as pl
from jax.experimental.pallas import tpu as pltpu
from jax.sharding import PartitionSpec as P

CHUNK = 64
QUAD = 4
LANES = QUAD * CHUNK
NEAR = 2 * CHUNK
MASKED = -1e30
OWN_FAR, OWN_NEAR, RIM_NEAR = 1.0, 2.0, 3.0
F32 = jnp.float32
BF16 = jnp.bfloat16
RING = 4
VMEM_LIMIT = 60 * 1024 * 1024


def halves(x):
    high = x.astype(BF16)
    return high, (x - high.astype(F32)).astype(BF16)


def mm(a, b):
    return jnp.dot(a, b, preferred_element_type=F32)


def mm_nt(a, b):
    return lax.dot_general(a, b, (((1,), (1,)), ((), ())), preferred_element_type=F32)


def softmaxes(logits, axis):
    upper = jnp.exp(logits - jnp.max(logits, axis=axis, keepdims=True))
    lower = jnp.exp(jnp.min(logits, axis=axis, keepdims=True) - logits)
    return (
        upper * (1.0 / jnp.sum(upper, axis=axis, keepdims=True)),
        lower * (1.0 / jnp.sum(lower, axis=axis, keepdims=True)),
    )


def softmax_grads(upper, lower, grad_upper, grad_lower, axis):
    return upper * (
        grad_upper - jnp.sum(upper * grad_upper, axis=axis, keepdims=True)
    ) - lower * (grad_lower - jnp.sum(lower * grad_lower, axis=axis, keepdims=True))


def keep(seg_ref, chunk):
    same = seg_ref[CHUNK * (chunk + 1) - 1] == seg_ref[CHUNK * (chunk + 2) - 1]
    return jnp.where(same, 1.0, 0.0).astype(F32)


def side(first, count, piece):
    return piece[:, first : first + count].reshape(-1, piece.shape[2])


def block_kernel(
    chunks, seg_ref, key_ref, value_ref, map_ref, seg_row_ref, state_ref, piece_ref
):
    upper, lower = softmaxes(mm(key_ref[...], map_ref[0]), 1)
    high, low = halves(jnp.concatenate([upper, lower], 1))
    values = value_ref[...].astype(F32)
    total = None
    for c in range(chunks):
        own = slice(CHUNK * c, CHUNK * (c + 1))
        tail = seg_row_ref[c, :, :CHUNK] == seg_ref[CHUNK * (c + 1) - 1]
        turned = jnp.concatenate([values[own].T, jnp.ones((16, CHUNK), F32)], 0)
        turned = jnp.where(tail, turned, 0.0).astype(BF16)
        state = mm(
            jnp.concatenate([turned, turned], 1), jnp.concatenate([high[own], low[own]], 0)
        )[: state_ref.shape[2]]
        state_ref[0, c] = state
        total = state if c == 0 else state + keep(seg_ref, c - 1) * total
    cut_up(total, seg_ref, piece_ref)


def key_kernel(
    chunks, window_ref, key_ref, value_ref, map_ref, seg_col_ref, seg_row_ref,
    feat_high_ref, feat_low_ref, feat_t_ref, value_t_ref, value_pair_ref, kind_ref,
):
    reach = window_ref[pl.program_id(0)]
    upper, lower = softmaxes(mm(key_ref[...], map_ref[0]), 1)
    features = jnp.concatenate([upper, lower], 1)
    high, low = halves(features)
    feat_high_ref[0] = high
    feat_low_ref[0] = low
    values = value_ref[...]
    value_pair_ref[0] = jnp.concatenate([values, values], 1)
    wide_values = values.astype(F32)
    for c in range(chunks):
        rows = slice(CHUNK * c, CHUNK * c + NEAR)
        turned_high, turned_low = halves(features[rows].T)
        feat_t_ref[0, c] = jnp.concatenate([turned_high, turned_low], 1)
        value_t = wide_values[rows].T.astype(BF16)
        value_t_ref[0, c] = jnp.concatenate([value_t, value_t], 1)
        near_row = lax.broadcasted_iota(jnp.int32, (NEAR, 128), 0)
        token = lax.broadcasted_iota(jnp.int32, (NEAR, 128), 1) % CHUNK
        distance = CHUNK + token - near_row
        same_doc = seg_col_ref[rows] == seg_row_ref[c, :, :128]
        inside = distance < reach
        own = near_row >= CHUNK
        kind = jnp.where(inside, jnp.where(own, OWN_NEAR, RIM_NEAR), jnp.where(own, OWN_FAR, 0.0))
        kind_ref[0, c] = jnp.where(same_doc & (distance >= 0), kind, 0.0).astype(BF16)


def kinds(kind_ref, c):
    kind = kind_ref[0, c].astype(F32)
    return jnp.concatenate([kind] * (LANES // 128), 1)


def signed(kind, linear):
    return jnp.where(kind == OWN_FAR, linear, jnp.where(kind == RIM_NEAR, -linear, 0.0))


def cut_up(total, seg_ref, piece_ref):
    share = piece_ref.shape[1] - 8
    width = total.shape[1]
    end = seg_ref[seg_ref.shape[0] - 1].astype(F32)
    extra = jnp.where(
        lax.broadcasted_iota(jnp.int32, (8, width), 0) == 0, total[128:136], end
    )
    for i in range(piece_ref.shape[0]):
        piece_ref[i, :share] = total[share * i : share * (i + 1)]
        piece_ref[i, share:] = extra


def whole_state(piece):
    share = piece.shape[1] - 8
    state = side(0, share, piece)
    norm = jnp.broadcast_to(piece[0, share : share + 1], (8, piece.shape[2]))
    return jnp.concatenate([state, norm], 0)


def scan_kernel(count, backward, piece_ref, out_ref):
    mark = piece_ref.shape[1] - 7
    total = jnp.zeros(piece_ref.shape[1:], F32)
    for position in range(count - 1, -1, -1) if backward else range(count):
        out_ref[position] = total
        piece = piece_ref[position]
        former = piece_ref[max(position - 1, 0), mark : mark + 1]
        total = piece + jnp.where(piece[mark : mark + 1] == former, total, 0.0)


def place_diagonal(blocks, diag_ref):
    for i, block in enumerate(blocks):
        diag_ref[i * CHUNK : (i + 1) * CHUNK, i * 128 : (i + 1) * 128] = block


def local_kernel(
    chunks, q0_ref, q1_ref, q2_ref, q3_ref, m0_ref, m1_ref, m2_ref, m3_ref, key_ref, high_ref,
    low_ref, value_t_ref, kind_ref, *refs,
):
    numer_ref, denom_ref, qf_high_ref, qf_low_ref, diag_ref = refs[-5:]

    @pl.when(pl.program_id(0) + pl.program_id(1) == 0)
    def _():
        diag_ref[...] = jnp.zeros_like(diag_ref)

    q_refs = (q0_ref, q1_ref, q2_ref, q3_ref)
    maps = jnp.concatenate([ref[0] for ref in (m0_ref, m1_ref, m2_ref, m3_ref)], 0)
    maps = maps.astype(F32).T.astype(BF16)
    every = range(chunks)
    near = [slice(CHUNK * c, CHUNK * c + NEAR) for c in every]
    blocks = [[ref[CHUNK * c : CHUNK * (c + 1)] for ref in q_refs] for c in every]
    for c in every:
        place_diagonal(blocks[c], diag_ref.at[c])
    logits = [mm_nt(maps, diag_ref[c]) for c in every]
    scores = [mm_nt(key_ref[near[c]], jnp.concatenate(blocks[c], 0)) for c in every]
    cuts = [halves(jnp.concatenate(softmaxes(logits[c], 0), 0)) for c in every]
    both = [
        mm(jnp.concatenate([high_ref[0, near[c]], low_ref[0, near[c]]], 0), cuts[c][0])
        for c in every
    ]
    third = [mm(high_ref[0, near[c]], cuts[c][1]) for c in every]
    for c in every:
        qf_high_ref[0, c], qf_low_ref[0, c] = cuts[c]
        kind = kinds(kind_ref, c)
        score = jnp.where(kind >= OWN_NEAR, scores[c] * 128 ** (-0.5), MASKED)
        weights = jnp.exp(score - jnp.max(score, axis=0, keepdims=True))
        linear = both[c][:NEAR] + both[c][NEAR:] + third[c]
        weights = weights + signed(kind, linear)
        denom_ref[0, c] = jnp.sum(weights, axis=0, keepdims=True)
        numer_ref[0, c] = mm(value_t_ref[0, c], jnp.concatenate(halves(weights), 0))


def enter_states(chunks, seg_ref, first_ref, state_ref, rows_ref, columns_ref, norm_ref):
    state = whole_state(first_ref)
    for c in range(chunks):
        if c > 0:
            state = state_ref[0, c - 1] + keep(seg_ref, c - 1) * state
        high, low = halves(jnp.concatenate([state, state[128:]], 0))
        rows_ref[c] = jnp.concatenate([high, low], 0)
        columns_ref[0, c] = jnp.concatenate(halves(state[:128].T), 1)
        norm_ref[0, c] = state[128:]


def output_kernel(
    chunks, seg_ref, t0_ref, t1_ref, t2_ref, t3_ref, numer_ref, denom_ref, qf_high_ref, qf_low_ref,
    first_ref, state_ref, value_pair_ref, kind_ref, seg_row_ref, right_ref,
    grad_denom_ref, key_grad_ref, state_grad_ref, piece_ref, columns_ref, norm_ref, rows_ref,
):
    begins = pl.program_id(1) + pl.program_id(2) == 0
    ends = (pl.program_id(1) == 1) & (pl.program_id(2) == pl.num_programs(2) - 1)

    @pl.when(begins)
    def _():
        enter_states(chunks, seg_ref, first_ref, state_ref, rows_ref, columns_ref, norm_ref)

    t_refs = (t0_ref, t1_ref, t2_ref, t3_ref)
    padded = rows_ref.shape[1] // 2
    every = range(chunks)
    carried = [
        jnp.where(seg_row_ref[c] == seg_ref[c * CHUNK + CHUNK - 1], 1.0, 0.0).astype(F32)
        for c in every
    ]
    both = [mm(rows_ref[c], qf_high_ref[0, c]) for c in every]
    third = [mm(rows_ref[c, :padded], qf_low_ref[0, c]) for c in every]
    cuts, grad_denoms = [], []
    for c in every:
        carry = (both[c][:padded] + both[c][padded:] + third[c]) * carried[c]
        inverse = 1.0 / (denom_ref[0, c] + carry[128:129])
        outputs = (numer_ref[0, c] + carry[:128]) * inverse
        targets = jnp.concatenate([ref[CHUNK * c : CHUNK * (c + 1)] for ref in t_refs], 0)
        residual = outputs - targets.astype(F32).T
        grad_denom = -jnp.sum(residual * outputs, axis=0, keepdims=True) * inverse
        grad_denom_ref[0, c] = grad_denom * carried[c]
        grad_denoms.append(grad_denom)
        cuts.append(halves(residual * inverse))
    linear = [
        mm(value_pair_ref[0, CHUNK * c : CHUNK * c + NEAR], jnp.concatenate(cuts[c], 0))
        for c in every
    ]
    left_high, left_low = [], []
    for c in every:
        linear_high, linear_low = halves(
            signed(kinds(kind_ref, c), linear[c] + grad_denoms[c])
        )
        mask = carried[c].astype(BF16)
        grad_high, grad_low = cuts[c][0] * mask, cuts[c][1] * mask
        right_ref[0, c] = jnp.concatenate([linear_high, linear_low, grad_high, grad_low], 0)
        denom_high, denom_low = halves(
            jnp.broadcast_to(grad_denoms[c] * carried[c], (16, LANES))
        )
        left_high.append(jnp.concatenate([linear_high, grad_high, denom_high], 0))
        left_low.append(jnp.concatenate([linear_low, grad_low, denom_low], 0))
    both = [
        mm_nt(jnp.concatenate([left_high[c], left_low[c]], 0), qf_high_ref[0, c]) for c in every
    ]
    third = [mm_nt(left_high[c], qf_low_ref[0, c]) for c in every]
    rows = NEAR + padded
    results = [both[c][:rows] + both[c][rows:] + third[c] for c in every]

    @pl.when(begins)
    def _():
        for c in range(chunks):
            key_grad_ref[0, c] = results[c][:NEAR]
            state_grad_ref[0, c] = results[c][NEAR : NEAR + 136]

    @pl.when(jnp.logical_not(begins))
    def _():
        for c in range(chunks):
            key_grad_ref[0, c] += results[c][:NEAR]
            state_grad_ref[0, c] += results[c][NEAR : NEAR + 136]

    @pl.when(ends)
    def _():
        total = state_grad_ref[0, chunks - 1]
        for c in range(chunks - 2, -1, -1):
            total = state_grad_ref[0, c] + keep(seg_ref, c) * total
        cut_up(total, seg_ref, piece_ref)


def query_kernel(
    chunks, core_ref, q0_ref, q1_ref, q2_ref, q3_ref, right_ref, grad_denom_ref, qf_high_ref,
    qf_low_ref, feat_t_ref, columns_ref, norm_ref, *refs,
):
    mine_ref, theirs_ref, diag_ref, left_ref, spread_ref = refs[-5:]

    @pl.when(pl.program_id(0) + pl.program_id(1) == 0)
    def _():
        diag_ref[...] = jnp.zeros_like(diag_ref)

    @pl.when(pl.program_id(1) == 0)
    def _():
        for c in range(chunks):
            feat_high, feat_low = feat_t_ref[0, c, :, :NEAR], feat_t_ref[0, c, :, NEAR:]
            state_high, state_low = columns_ref[0, c, :, :128], columns_ref[0, c, :, 128:]
            left_ref[c] = jnp.concatenate(
                [feat_high, feat_high, state_high, state_high, feat_low, state_low], 1
            )
            norm = jnp.broadcast_to(norm_ref[0, c, :1], (128, norm_ref.shape[3]))
            spread_ref[c] = norm.T

    q_refs = (q0_ref, q1_ref, q2_ref, q3_ref)
    every = range(chunks)
    for c in every:
        place_diagonal([ref[CHUNK * c : CHUNK * (c + 1)] for ref in q_refs], diag_ref.at[c])
    feature_grads = []
    for c in every:
        stack = right_ref[0, c]
        right = jnp.concatenate([stack, stack[:NEAR], stack[2 * NEAR : 2 * NEAR + 128]], 0)
        feature_grads.append(mm(left_ref[c], right))
    cuts = []
    for c in every:
        norm = jnp.concatenate([spread_ref[c]] * (LANES // 128), 1)
        feature_grad = feature_grads[c] + norm * grad_denom_ref[0, c]
        high, low = qf_high_ref[0, c], qf_low_ref[0, c]
        upper = high[:128].astype(F32) + low[:128].astype(F32)
        lower = high[128:].astype(F32) + low[128:].astype(F32)
        cuts.append(
            halves(softmax_grads(upper, lower, feature_grad[:128], feature_grad[128:], 0))
        )
    both = [mm(jnp.concatenate(cuts[c], 0), diag_ref[c]) for c in every]
    total = sum(x[:128] + x[128:] for x in both)

    for core, own in enumerate(((mine_ref, theirs_ref), (theirs_ref, mine_ref))):

        @pl.when(core_ref[0] == core)
        def _(own=own):
            for i in range(QUAD):
                own[i % 2][i // 2, 0] = total[:, i * 128 : (i + 1) * 128]


def tail_kernel(
    chunks, seg_ref, key_ref, value_ref, map_ref, seg_col_ref, later_ref, state_grad_ref,
    key_grad_ref, out_ref,
):
    logits = mm(key_ref[...], map_ref[0])
    upper, lower = softmaxes(logits, 1)
    values = value_ref[...]
    pieces = [key_grad_ref[0, 0, :CHUNK]]
    leaving = whole_state(later_ref)
    states = []
    for c in range(chunks - 1, -1, -1):
        states.append(leaving)
        leaving = state_grad_ref[0, c] + keep(seg_ref, c) * leaving
    states = states[::-1]
    for c in range(chunks):
        own = slice(CHUNK * (c + 1), CHUNK * (c + 2))
        grads = key_grad_ref[0, c, CHUNK:]
        if c + 1 < chunks:
            grads = grads + key_grad_ref[0, c + 1, :CHUNK]
        tail = jnp.where(seg_col_ref[own] == seg_ref[CHUNK * (c + 2) - 1], 1.0, 0.0).astype(F32)
        entry_high, entry_low = halves(states[c][:128])
        through = mm(
            jnp.concatenate([values[own], values[own]], 1),
            jnp.concatenate([entry_high, entry_low], 0),
        )
        pieces.append(grads + tail * (through + states[c][128:129]))
    grads = jnp.concatenate(pieces, 0)
    logit_grad = softmax_grads(upper, lower, grads[:, :128], grads[:, 128:], 1)
    turned = key_ref[...].astype(F32).T.astype(BF16)
    out_ref[0] = mm(
        jnp.concatenate([turned, turned], 1), jnp.concatenate(halves(logit_grad), 0)
    )


def call(
    kernel, name, microseconds, grid, in_specs, out_specs, out_shape, args, scalars=0, scratch=(),
    aliases=None,
):
    return pl.pallas_call(
        kernel,
        grid_spec=pltpu.PrefetchScalarGridSpec(
            num_scalar_prefetch=scalars,
            grid=grid,
            in_specs=in_specs,
            out_specs=out_specs,
            scratch_shapes=scratch,
        ),
        out_shape=out_shape,
        compiler_params=pltpu.CompilerParams(vmem_limit_bytes=VMEM_LIMIT),
        cost_estimate=pl.CostEstimate(
            flops=int(microseconds * 1e9), bytes_accessed=int(microseconds * 3e6), transcendentals=0
        ),
        input_output_aliases=aliases or {},
        name=name,
    )(*args)


def exchange(pieces, axis):
    return lax.all_to_all(pieces, axis, 0, 0, tiled=True)


def on_device(queries, keys, values, targets, segments, window, query_feature_projection, key_map):
    head_count, head_dim, map_width = query_feature_projection.shape
    groups = key_map.shape[0]
    tok_rows = queries.shape[1]
    near_rows = tok_rows + CHUNK
    chunks = tok_rows // CHUNK
    features = 2 * map_width
    quads = head_count // groups // QUAD // 2
    ctx, dp = lax.axis_size("ctx"), lax.axis_size("dp")
    me = lax.axis_index("ctx")
    state_rows = head_dim + 8
    sds = jax.ShapeDtypeStruct

    seg_row = segments[0]
    seg_rows = jnp.tile(seg_row.reshape(chunks, 1, CHUNK), (1, 1, QUAD))
    query_rows, target_rows = queries[0], targets[0]
    group_spec = lambda *shape: pl.BlockSpec((1,) + shape, lambda g, *_: (g,) + (0,) * len(shape))
    whole = lambda shape: pl.BlockSpec(shape, lambda *_: (0,) * len(shape))
    column = lambda rows: pl.BlockSpec((rows, head_dim), lambda g, *_: (0, g))
    per_group = ctx // groups
    piece_shape = (ctx, head_dim // per_group + 8, features)
    piece_spec = pl.BlockSpec((per_group,) + piece_shape[1:], lambda g, *_: (g, 0, 0))

    chunk_state, block_pieces = call(
        functools.partial(block_kernel, chunks), "block", 4, (groups,),
        [
            column(tok_rows), column(tok_rows), group_spec(head_dim, map_width),
            whole((chunks, 1, LANES)),
        ],
        [group_spec(chunks, state_rows, features), piece_spec],
        [sds((groups, chunks, state_rows, features), F32), sds(piece_shape, F32)],
        (seg_row, keys[0], values[0], key_map, seg_rows),
        scalars=1,
    )

    def across(pieces, backward, first, second):
        received, aside = lax.optimization_barrier((exchange(pieces, "ctx"), first()))
        summed = call(
            functools.partial(scan_kernel, ctx, backward), "scan", 2, (1,), [whole(piece_shape)],
            whole(piece_shape), sds(piece_shape, F32), (received,),
        )
        summed, aside = lax.optimization_barrier((summed, aside))
        done, free = second(aside)
        return *lax.optimization_barrier((exchange(summed, "ctx"), done)), free

    block_pieces, row_keys, row_values = lax.optimization_barrier(
        (block_pieces, keys[0], values[0])
    )
    rim = jnp.concatenate([row_keys[-CHUNK:], row_values[-CHUNK:]], 1)
    rim_seg = jnp.broadcast_to(seg_row[-CHUNK:].astype(BF16)[:, None], (CHUNK, 128))
    rim = lax.ppermute(
        jnp.concatenate([rim, rim_seg], 1), "ctx", [(i, i + 1) for i in range(ctx - 1)]
    )
    width = keys.shape[2]
    near_keys = jnp.concatenate([rim[:, :width], row_keys], 0)
    near_values = jnp.concatenate([rim[:, width : 2 * width], row_values], 0)
    rim_segments = jnp.where(me > 0, rim[:, 2 * width].astype(jnp.int32), -1)
    near_segments = jnp.concatenate([rim_segments, seg_row], 0)
    seg_col = near_segments[:, None]
    feat_high, feat_low, feat_t, value_t, value_pair, kind = call(
        functools.partial(key_kernel, chunks), "keys", 5, (groups,),
        [
            column(near_rows), column(near_rows), group_spec(head_dim, map_width),
            whole((near_rows, 1)), whole((chunks, 1, LANES)),
        ],
        [
            group_spec(near_rows, features), group_spec(near_rows, features),
            group_spec(chunks, features, 2 * NEAR), group_spec(chunks, head_dim, 2 * NEAR),
            group_spec(near_rows, 2 * head_dim), group_spec(chunks, NEAR, 128),
        ],
        [
            sds((groups, near_rows, features), BF16), sds((groups, near_rows, features), BF16),
            sds((groups, chunks, features, 2 * NEAR), BF16),
            sds((groups, chunks, head_dim, 2 * NEAR), BF16),
            sds((groups, near_rows, 2 * head_dim), BF16),
            sds((groups, chunks, NEAR, 128), BF16),
        ],
        (window, near_keys, near_values, key_map, seg_col, seg_rows),
        scalars=1,
    )

    half_steps = groups * quads
    steps = 2 * half_steps
    grid = (groups, quads)
    spot = lambda g, q: g * quads + q

    def step_spec(half, *shape):
        return pl.BlockSpec(
            (1,) + shape, lambda g, q, *_: (half * half_steps + spot(g, q),) + (0,) * len(shape)
        )

    def head_specs(half):
        return [
            pl.BlockSpec(
                (tok_rows, head_dim), lambda g, q, *_, i=i: (0, (spot(g, q) * QUAD + i) * 2 + half)
            )
            for i in range(QUAD)
        ]

    def local(half, so_far):
        map_specs = [
            pl.BlockSpec(
                (1, head_dim, map_width),
                lambda g, q, *_, i=i: ((spot(g, q) * QUAD + i) * 2 + half, 0, 0),
            )
            for i in range(QUAD)
        ]
        step = functools.partial(step_spec, half)
        return call(
            functools.partial(local_kernel, chunks), "local", 15, grid,
            head_specs(half) + map_specs
            + [
                column(near_rows), group_spec(near_rows, features),
                group_spec(near_rows, features), group_spec(chunks, head_dim, 2 * NEAR),
                group_spec(chunks, NEAR, 128),
            ]
            + [pl.BlockSpec(memory_space=pl.ANY)] * len(so_far),
            [
                step(chunks, head_dim, LANES), step(chunks, 1, LANES),
                step(chunks, features, LANES), step(chunks, features, LANES),
            ],
            [
                sds((steps, chunks, head_dim, LANES), F32), sds((steps, chunks, 1, LANES), F32),
                sds((steps, chunks, features, LANES), BF16),
                sds((steps, chunks, features, LANES), BF16),
            ],
            (
                *([query_rows] * QUAD), *([query_feature_projection] * QUAD), near_keys, feat_high,
                feat_low, value_t, kind, *so_far,
            ),
            scratch=[pltpu.VMEM((chunks, LANES, QUAD * head_dim), BF16)],
            aliases={13 + i: i for i in range(len(so_far))},
        )

    entering, forward, _ = across(
        block_pieces, False, lambda: local(0, ()), lambda so_far: (local(1, so_far), None)
    )

    every_step = lambda *shape: pl.BlockSpec(
        (1,) + shape, lambda g, h, q, *_: (h * half_steps + spot(g, q),) + (0,) * len(shape)
    )
    right, grad_denom, key_grad, state_grad, grad_pieces, columns, norms = call(
        functools.partial(output_kernel, chunks), "outputs", 45, (groups, 2, quads),
        [
            pl.BlockSpec(
                (tok_rows, head_dim),
                lambda g, h, q, *_, i=i: (0, (spot(g, q) * QUAD + i) * 2 + h),
            )
            for i in range(QUAD)
        ]
        + [
            every_step(chunks, head_dim, LANES), every_step(chunks, 1, LANES),
            every_step(chunks, features, LANES), every_step(chunks, features, LANES),
            piece_spec, group_spec(chunks, state_rows, features),
            group_spec(near_rows, 2 * head_dim), group_spec(chunks, NEAR, 128),
            whole((chunks, 1, LANES)),
        ],
        [
            every_step(chunks, 4 * NEAR, LANES), every_step(chunks, 1, LANES),
            group_spec(chunks, NEAR, features), group_spec(chunks, state_rows, features),
            piece_spec, group_spec(chunks, features, 2 * head_dim), group_spec(chunks, 8, features),
        ],
        [
            sds((steps, chunks, 4 * NEAR, LANES), BF16), sds((steps, chunks, 1, LANES), F32),
            sds((groups, chunks, NEAR, features), F32),
            sds((groups, chunks, state_rows, features), F32), sds(piece_shape, F32),
            sds((groups, chunks, features, 2 * head_dim), BF16),
            sds((groups, chunks, 8, features), F32),
        ],
        (
            near_segments, *([target_rows] * QUAD), *forward, entering, chunk_state, value_pair,
            kind, seg_rows,
        ),
        scalars=1,
        scratch=[pltpu.VMEM((chunks, 2 * (state_rows + 8), features), BF16)],
    )

    core = lax.rem(me, 2)
    partner = [(i, i ^ 1) for i in range(ctx)]

    def query(half, right, start, count, so_far=()):
        part = pl.BlockSpec(
            (QUAD // 2, 1, map_width, head_dim), lambda g, q, *_: (q, g + start, 0, 0)
        )
        shape = sds((RING, RING, map_width, head_dim), F32)
        from_start = lambda spec: pl.BlockSpec(
            spec.block_shape, lambda g, q, *_: spec.index_map(g + start, q)
        )
        step = functools.partial(step_spec, half)
        specs = head_specs(half) + [
            step(chunks, 4 * NEAR, LANES), step(chunks, 1, LANES), step(chunks, features, LANES),
            step(chunks, features, LANES), group_spec(chunks, features, 2 * NEAR),
            group_spec(chunks, features, 2 * head_dim), group_spec(chunks, 8, features),
        ]
        return call(
            functools.partial(query_kernel, chunks), "queries", 10 * count // groups,
            (count, quads),
            [from_start(spec) for spec in specs]
            + [pl.BlockSpec(memory_space=pl.ANY)] * len(so_far),
            [part, part], [shape, shape],
            (
                core[None], *([query_rows] * QUAD), right, grad_denom, *forward[2:], feat_t,
                columns, norms, *so_far,
            ),
            scalars=1,
            scratch=[
                pltpu.VMEM((chunks, LANES, QUAD * head_dim), BF16),
                pltpu.VMEM((chunks, features, 6 * 128), BF16),
                pltpu.VMEM((chunks, features, 128), F32),
            ],
            aliases={12 + i: i for i in range(len(so_far))},
        )

    place = {"z": me // 2 % RING, "x": me // (2 * RING)}

    def routes(axis):
        if axis == "dp":
            return [[(i, (i + s) % dp) for i in range(dp)] for s in range(1, RING)]
        stride = 2 if axis == "z" else 2 * RING
        at = lambda i, s: i + ((i // stride + s) % RING - i // stride % RING) * stride
        return [[(i, at(i, s)) for i in range(ctx)] for s in range(1, RING)]

    def add_up(own, one, two, three):
        return (own + two) + (one + three)

    def around(axis, value):
        name = axis if axis == "dp" else "ctx"
        return add_up(value, *(lax.ppermute(value, name, route) for route in routes(axis)))

    def slice_around(axis, dim, *values):
        own, *others = [
            sum(
                lax.dynamic_index_in_dim(value, lax.rem(place[axis] + s, RING), dim, False)
                for value in values
            )
            for s in range(RING)
        ]
        return add_up(
            own, *(lax.ppermute(part, "ctx", route) for part, route in zip(others, routes(axis)))
        )

    def over_chip(mine, theirs):
        return mine, lax.ppermute(theirs, "ctx", partner)

    def second_half(done):
        first, right = lax.optimization_barrier((over_chip(*done[0]), done[1]))
        return query(1, right, 0, groups), slice_around("z", 0, *first)

    later, second, first = across(
        grad_pieces, True, lambda: (query(0, right, 0, groups), right), second_half
    )

    key_grad = call(
        functools.partial(tail_kernel, chunks), "tail", 5, (groups,),
        [
            column(near_rows), column(near_rows), group_spec(head_dim, map_width),
            whole((near_rows, 1)), piece_spec, group_spec(chunks, state_rows, features),
            group_spec(chunks, NEAR, features),
        ],
        group_spec(head_dim, map_width), sds((groups, head_dim, map_width), F32),
        (
            near_segments, near_keys, near_values, key_map, seg_col, later, state_grad, key_grad,
        ),
        scalars=1,
    )

    key_grad, first = lax.optimization_barrier((key_grad, first))
    key_halves = key_grad.reshape(2, -1, map_width)
    key_mine = lax.dynamic_index_in_dim(key_halves, core, 0, False)
    key_theirs = lax.dynamic_index_in_dim(key_halves, 1 - core, 0, False)
    key_mine, key_theirs = over_chip(key_mine, key_theirs)
    second = over_chip(*second)
    key_sum, second = lax.optimization_barrier((key_mine + key_theirs, second))
    key_sum = around("z", around("dp", around("x", key_sum)))
    second = slice_around("x", 0, slice_around("z", 0, *second))
    first = slice_around("x", 0, first)
    both = around("dp", jnp.stack([first, second], 0))
    key_theirs = lax.ppermute(key_sum, "ctx", partner)
    full_key = jnp.concatenate(
        [jnp.where(core == 0, key_sum, key_theirs), jnp.where(core == 0, key_theirs, key_sum)], 0
    )
    return (both.transpose(0, 2, 1), full_key.reshape(groups, head_dim, map_width))


def solution(mesh):
    return jax.shard_map(
        on_device,
        mesh=mesh,
        in_specs=(
            P("dp", "ctx", None),
            P("dp", "ctx", None),
            P("dp", "ctx", None),
            P("dp", "ctx", None),
            P("dp", "ctx"),
            P(),
            P(),
            P(),
        ),
        out_specs=(P("ctx", None, None), P()),
        check_vma=False,
    )
```
